256 devices in a mesh: group: 32 (over y, x, core), tensor: 8 (over z).
Axes of the slice: x: 4, y: 4, z: 8, core: 2. Of those that a mesh axis runs over, the one named last changes fastest.
Arguments:
- hidden: bfloat16 [32, 2, 256, 4096], P('group', None, 'tensor'), may hold values from -6 to 6
- norm_gain: bfloat16 [4096], replicated, may hold values from 0.5 to 1.5
- w_query: bfloat16 [4096, 4096], P(None, 'tensor'), may hold values from -0.09375 to 0.09375
- w_key: bfloat16 [4096, 1024], P(None, 'tensor'), may hold values from -0.09375 to 0.09375
- w_value: bfloat16 [4096, 1024], P(None, 'tensor'), may hold values from -0.09375 to 0.09375
- w_output: bfloat16 [4096, 4096], P('tensor'), may hold values from -0.09375 to 0.09375
- prefix_pool: bfloat16 [65536, 8, 2048], P('group', None, 'tensor'), may hold values from -120 to 120
- page_table: int32 [32, 2, 1024], P('group'), may hold values from 0 to 1023, each once within a row
- prefix_len: int32 [32, 2], replicated, may hold values from 1024 to 8192
- source: int32 [32], replicated, may hold values from 0 to 31, as said below
- decode_owner: int32 [32, 32], replicated, may hold values from 0 to 31, as said below
Outputs:
- layer_out: bfloat16 [8192, 4096], P(('group', 'tensor'))
- decode_pool: bfloat16 [1024, 8, 2048], P('group', None, 'tensor')
The draws below stay inside these ranges and needn't reach their ends.
Inputs may be any that keep to these rules, and one draw needn't show every extreme that they name: source[h] is h or h - 1 modulo 32. For each page index k, the values decode_owner[h, k] over all h are all different; no row names one group more than 2 times, and some row names a group exactly 2 times.
All inputs are finite; a program needn't handle non-finite values.
Results may differ from the reference program's by a relative error of at most 0.012.
Values may be sent and summed in bfloat16 or wider, within the bound.
No kernel may reach another device: no remote copies, remote signals or barrier semaphores. Data moves between devices by JAX's collectives and lax.ppermute only.
A program may use at most 128 MiB of HBM per device.

```python
import math
import jax
import jax.numpy as jnp
from jax import lax

D = 4096
HQ = 32
KVH = 8
HD = 128
PAGE = 8
BLOCK = 256
PREFIX = 8192
GROUPS = 32
NPAGE = 32
PREF_PAGES = 1024
KV_COLS = 2048
N_TENSOR = 8


def draw_prefix_pool(key, part):
    values = jax.random.normal(key, (GROUPS * 2 * PREF_PAGES, PAGE, KV_COLS), jnp.float32)
    values = jnp.clip(values, -5.0, 5.0)
    return values.astype(jnp.bfloat16)


def draw_source(key, part):
    indices = jnp.arange(GROUPS)
    coins = jax.random.randint(jax.random.fold_in(key, 2), (GROUPS,), 0, 2)
    middle = GROUPS // 2
    forced = (indices == 0) | (indices == middle)
    takes = jnp.logical_or(forced, coins == 1)
    picked = jnp.where(takes, indices - 1, indices)
    return (picked % GROUPS).astype(jnp.int32)


def draw_decode_owner(key, part):
    spread_count = min(GROUPS, NPAGE - NPAGE // 4)
    offsets_all = jax.random.permutation(jax.random.fold_in(key, 1), GROUPS)
    relabel = jax.random.permutation(jax.random.fold_in(key, 2), GROUPS)
    offsets = offsets_all[jnp.arange(NPAGE) % spread_count]
    indices = jnp.arange(GROUPS)
    return relabel[(indices[:, None] + offsets[None, :]) % GROUPS].astype(jnp.int32)


def touch_ends(result, rng, low, high):
    shape = result.shape
    place = [jax.random.randint(jax.random.fold_in(rng, axis), (), 0, shape[axis]) for axis in range(len(shape))]
    result = result.at[tuple(place)].set(low)
    longest = shape.index(max(shape))
    place[longest] = (place[longest] + 1) % shape[longest]
    return result.at[tuple(place)].set(high)


def block_levels(rng, dims, pieces, least, top_value):
    def one(position, shards_of):
        heights = jax.random.uniform(jax.random.fold_in(jax.random.fold_in(rng, 6), position), (shards_of,), jnp.float32, least / len(pieces), top_value / len(pieces))
        return jnp.repeat(jnp.exp(heights), dims[position] // shards_of).reshape((-1,) + (1,) * (len(dims) - position - 1))

    factor_of = one(*pieces[0])
    for cut in pieces[1:]:
        factor_of = factor_of * one(*cut)
    return factor_of


def scatter_about(key, extent, width, most, pieces=(), held_as=jnp.bfloat16):
    drawn = jax.random.normal(key, extent, jnp.float32) * width
    if len(pieces) > 0:
        drawn = block_levels(key, extent, pieces, -0.22, 0.18) * drawn
    return jnp.clip(drawn, min=-most, max=most).astype(held_as)


def setup_inputs(seed: int = 0) -> dict:
    arg_keys = jax.random.split(jax.random.key(seed), 12)
    hidden = scatter_about(arg_keys[0], (GROUPS, 2, BLOCK, D), 1.0, 6.0, ((0, 32), (2, 8)))
    norm_gain = jnp.clip(1.0 + 0.1 * jax.random.normal(arg_keys[1], (D,), jnp.float32), 0.5, 1.5).astype(jnp.bfloat16)
    w_query = scatter_about(arg_keys[2], (D, HQ * HD), D ** -0.5, 0.09375, ((1, 8),))
    w_key = scatter_about(arg_keys[3], (D, KVH * HD), D ** -0.5, 0.09375, ((1, 8),))
    w_value = scatter_about(arg_keys[4], (D, KVH * HD), D ** -0.5, 0.09375, ((1, 8),))
    w_output = scatter_about(arg_keys[5], (HQ * HD, D), (HQ * HD) ** -0.5, 0.09375, ((0, 8),))
    prefix_pool = draw_prefix_pool(jax.random.fold_in(arg_keys[11], 71), 0)
    page_table = jax.vmap(lambda own: jax.random.permutation(own, PREF_PAGES))(jax.random.split(arg_keys[7], GROUPS * 2)).reshape((GROUPS, 2, PREF_PAGES)).astype(jnp.int32)
    prefix_len = touch_ends(jax.random.randint(arg_keys[8], (GROUPS, 2), PREFIX // 8, PREFIX + 1), jax.random.fold_in(arg_keys[8], 1), PREFIX // 8, PREFIX).astype(jnp.int32)
    source = draw_source(jax.random.fold_in(arg_keys[11], 71), 0)
    decode_owner = draw_decode_owner(jax.random.fold_in(arg_keys[11], 71), 0)
    return {"hidden": hidden, "norm_gain": norm_gain, "w_query": w_query, "w_key": w_key, "w_value": w_value, "w_output": w_output, "prefix_pool": prefix_pool, "page_table": page_table, "prefix_len": prefix_len, "source": source, "decode_owner": decode_owner}


EPS = 1e-05
THETA = 500000.0

def rotate(values, positions):
    half_dim = values.shape[-1] // 2
    frequency = THETA ** (-(jnp.arange(half_dim, dtype=jnp.float32) * 2.0) / values.shape[-1])
    angles = positions[..., None] * frequency
    cosine = jnp.cos(angles)[..., None, :]
    sines = jnp.sin(angles)[..., None, :]
    first_half = values[..., :half_dim]
    second = values[..., half_dim:]
    return jnp.concatenate([first_half * cosine - second * sines, second * cosine + first_half * sines], axis=-1)

def reference(hidden, norm_gain, w_query, w_key, w_value, w_output, prefix_pool, page_table, prefix_len, source, decode_owner):
    group_size = HQ // KVH
    score_scale = 1.0 / math.sqrt(HD)
    flat_hidden = hidden.reshape(GROUPS * 2, BLOCK, D)
    flat_table = page_table.reshape(GROUPS * 2, PREF_PAGES)
    flat_len = prefix_len.reshape(GROUPS * 2)

    def one_group(slot_index):
        owner_group = source[slot_index].astype(jnp.int32)
        slot = jnp.where(owner_group == slot_index, 0, 1).astype(jnp.int32)
        entry = (owner_group * 2 + slot).astype(jnp.int32)
        prefix_count = flat_len[entry]
        block_rows = lax.dynamic_slice_in_dim(flat_hidden, entry, 1, 0)[0]
        block_f32 = block_rows.astype(jnp.float32)
        mean_square = lax.optimization_barrier(jnp.mean(block_f32 * block_f32, axis=-1, keepdims=True))
        normed = (block_f32 * lax.rsqrt(mean_square + EPS) * norm_gain.astype(jnp.float32)).astype(jnp.bfloat16)
        queries = jnp.dot(normed, w_query, preferred_element_type=jnp.float32).reshape(BLOCK, HQ, HD)
        new_keys = jnp.dot(normed, w_key, preferred_element_type=jnp.float32).reshape(BLOCK, KVH, HD)
        new_values = jnp.dot(normed, w_value, preferred_element_type=jnp.float32).reshape(BLOCK, KVH, HD).astype(jnp.bfloat16)
        positions = (prefix_count + jnp.arange(BLOCK, dtype=jnp.int32)).astype(jnp.float32)
        queries = rotate(queries, positions).astype(jnp.bfloat16)
        new_keys = rotate(new_keys, positions).astype(jnp.bfloat16)
        slot_order = lax.dynamic_slice_in_dim(flat_table, entry, 1, 0)[0].astype(jnp.int32)
        prefix_kv = jnp.take(prefix_pool, entry * PREF_PAGES + slot_order, axis=0)
        prefix_kv = prefix_kv.reshape(PREFIX, KVH, 2, HD)
        all_keys = jnp.concatenate([prefix_kv[:, :, 0], new_keys], axis=0)
        values = jnp.concatenate([prefix_kv[:, :, 1], new_values], axis=0)
        column = jnp.arange(PREFIX + BLOCK, dtype=jnp.int32)[None, :]
        row_index = jnp.arange(BLOCK, dtype=jnp.int32)[:, None]
        allowed = jnp.where(column < PREFIX, column < prefix_count, column - PREFIX <= row_index)
        grouped = queries.reshape(BLOCK, KVH, group_size, HD).astype(jnp.float32)
        scores = jnp.einsum('qhgd,khd->hgqk', grouped, all_keys.astype(jnp.float32)) * score_scale
        scores = jnp.where(allowed, scores, -jnp.inf)
        row_max = lax.optimization_barrier(jnp.max(scores, axis=-1, keepdims=True))
        exp_scores = jnp.where(allowed, jnp.exp(scores - row_max), 0.0)
        row_total = lax.optimization_barrier(jnp.sum(exp_scores, axis=-1))
        weights = exp_scores.astype(jnp.bfloat16)
        mixed_heads = jnp.einsum('hgqk,khd->qhgd', weights.astype(jnp.float32), values.astype(jnp.float32))
        attended = (mixed_heads / jnp.transpose(row_total, (2, 0, 1))[..., None]).astype(jnp.bfloat16)
        blocks = attended.reshape(BLOCK, N_TENSOR, HQ * HD // N_TENSOR).astype(jnp.float32)
        projections = w_output.reshape(N_TENSOR, HQ * HD // N_TENSOR, D).astype(jnp.float32)
        partial_value = jnp.einsum('qtc,tcd->tqd', blocks, projections).astype(jnp.bfloat16)
        summed = lax.optimization_barrier(jnp.sum(partial_value.astype(jnp.float32), axis=0))
        out_rows = (block_f32 + summed).astype(jnp.bfloat16)
        new_kv = jnp.stack([new_keys, new_values], axis=2).reshape(BLOCK, KV_COLS)
        return (out_rows, new_kv)
    block_outs, block_kv = lax.map(one_group, jnp.arange(GROUPS, dtype=jnp.int32))
    layer_out = block_outs.reshape(GROUPS * BLOCK, D)
    page_rows = block_kv.reshape(GROUPS * NPAGE, PAGE, KV_COLS)
    pool_slots = (decode_owner.astype(jnp.int32) * NPAGE + jnp.arange(NPAGE, dtype=jnp.int32)[None, :]).reshape(-1)
    kv_pool = jnp.zeros((GROUPS * NPAGE, PAGE, KV_COLS), jnp.bfloat16).at[pool_slots].set(page_rows)
    return (layer_out, kv_pool)
```

```python
import functools
import math

import jax
import jax.numpy as jnp
from jax import lax
from jax.experimental import pallas as pl
from jax.experimental.pallas import tpu as pltpu
from jax.sharding import PartitionSpec as P

HD = 128
PAGE = 8
BLOCK = 256
PREFIX = 8192
EPS = 1e-05
THETA = 500000.0

NT = 8
HEADS = 4
SHARD = BLOCK // NT
TILE = 256
KBLK = 1024
NKB = PREFIX // KBLK
KEYS = PREFIX + BLOCK
NCH = 4
CHROWS = PREFIX // NCH
MASKED = -1e30
EXP_SCALE = math.log2(math.e) / math.sqrt(HD)
MIB = 1 << 20
F32 = jnp.float32
BF16 = jnp.bfloat16

VMEM = pl.BlockSpec(memory_space=pltpu.VMEM)
SMEM = pl.BlockSpec(memory_space=pltpu.SMEM)
ANY = pl.BlockSpec(memory_space=pl.ANY)


def shift(value, axis, distance):
    count = lax.axis_size(axis)
    return lax.ppermute(value, axis, [(i, (i + distance) % count) for i in range(count)])


def norm_kernel(take_ref, own_ref, handed_ref, gain_ref, rows_ref, normed_ref):
    take = take_ref[0] != 0
    rows = jnp.where(take, handed_ref[...].astype(F32), own_ref[...].astype(F32))
    rows_ref[...] = rows.astype(BF16)
    mean_square = jnp.mean(rows * rows, axis=-1, keepdims=True)
    normed_ref[...] = (rows * lax.rsqrt(mean_square + EPS) * gain_ref[...].astype(F32)).astype(BF16)


def choose_and_norm(take, own, handed, gain):
    return pl.pallas_call(
        norm_kernel,
        out_shape=[jax.ShapeDtypeStruct(own.shape, BF16)] * 2,
        in_specs=[SMEM, VMEM, VMEM, VMEM],
        out_specs=[VMEM, VMEM],
        compiler_params=pltpu.CompilerParams(vmem_limit_bytes=8 * MIB),
        cost_estimate=pl.CostEstimate(flops=10**6, bytes_accessed=10**6, transcendentals=0),
        name="choose_and_norm",
    )(take, own, handed, gain)


def qkv_kernel(z_ref, *refs):
    shards = refs[:NT]
    cos_ref, sin_ref, wq_hbm, wk_hbm, wv_hbm, q_ref, kv_ref, x_ref, wq_ref, wk_ref, wv_ref, sems = refs[NT:]
    copies = [
        pltpu.make_async_copy(src, dst, sems.at[n])
        for n, (src, dst) in enumerate([(wk_hbm, wk_ref), (wv_hbm, wv_ref)])
    ]
    half = wq_hbm.shape[0] // 2
    copies += [
        pltpu.make_async_copy(wq_hbm.at[pl.ds(n * half, half)], wq_ref.at[pl.ds(n * half, half)], sems.at[2 + n])
        for n in range(2)
    ]
    for copy in copies:
        copy.start()
    z = z_ref[0]
    for relative, shard in enumerate(shards):
        place = lax.rem(z + relative, NT)
        x_ref[pl.ds(pl.multiple_of(place * SHARD, SHARD), SHARD), :] = shard[...]
    cosine = cos_ref[...]
    sine = sin_ref[...]

    def rotated(values):
        return values * cosine + pltpu.roll(values, HD // 2, 1) * sine

    copies[0].wait()
    kv_ref[:, :HD] = rotated(jnp.dot(x_ref[...], wk_ref[...], preferred_element_type=F32)).astype(BF16)
    copies[1].wait()
    kv_ref[:, HD:] = jnp.dot(x_ref[...], wv_ref[...], preferred_element_type=F32).astype(BF16)
    copies[2].wait()
    copies[3].wait()
    for pair in range(HEADS // 2):
        both = jnp.dot(x_ref[...], wq_ref[:, pair * 2 * HD : (pair + 1) * 2 * HD], preferred_element_type=F32)
        for one in range(2):
            head = rotated(both[:, one * HD : (one + 1) * HD]).astype(BF16)
            n = pair * 2 + one
            for shard in range(NT):
                q_ref[shard, n * SHARD : (n + 1) * SHARD, :] = head[shard * SHARD : (shard + 1) * SHARD, :]


def project(z, shards, cosine, sine, w_query, w_key, w_value):
    depth, query_width = w_query.shape
    return pl.pallas_call(
        qkv_kernel,
        out_shape=[
            jax.ShapeDtypeStruct((NT, HEADS * SHARD, HD), BF16),
            jax.ShapeDtypeStruct((BLOCK, 2 * HD), BF16),
        ],
        in_specs=[SMEM] + [VMEM] * (NT + 2) + [ANY] * 3,
        out_specs=[VMEM, VMEM],
        scratch_shapes=[
            pltpu.VMEM((BLOCK, depth), BF16),
            pltpu.VMEM(w_query.shape, BF16),
            pltpu.VMEM(w_key.shape, BF16),
            pltpu.VMEM(w_value.shape, BF16),
            pltpu.SemaphoreType.DMA((4,)),
        ],
        compiler_params=pltpu.CompilerParams(vmem_limit_bytes=28 * MIB),
        cost_estimate=pl.CostEstimate(
            flops=2 * BLOCK * depth * (query_width + 2 * HD), bytes_accessed=9 * 10**6, transcendentals=0
        ),
        name="project",
    )(z, *shards, cosine, sine, w_query, w_key, w_value)


def attention_kernel(tiles, picks, info_ref, q_ref, new_ref, bias_ref, wo_hbm, pool_hbm, *refs):
    handed = refs[:NCH]
    out_ref, kv_ref, s_ref, att_ref, wo_ref, kv_sem, wo_sem = refs[NCH:]
    z = info_ref[0]
    take = info_ref[1]

    def cache_copy(n, source):
        return pltpu.make_async_copy(source, kv_ref.at[pl.ds(n * CHROWS, CHROWS)], kv_sem.at[n])

    @pl.when(take != 0)
    def _():
        for n in range(NCH):
            cache_copy(n, handed[n]).start()

    @pl.when(take == 0)
    def _():
        for n in range(NCH):
            cache_copy(n, pool_hbm.at[pl.ds(n * CHROWS, CHROWS)]).start()

    wo_copy = pltpu.make_async_copy(wo_hbm, wo_ref, wo_sem)
    wo_copy.start()

    def shard_of(tile, half):
        return lax.rem(z + picks[2 * tile + half], NT)

    def query_tile(tile):
        return jnp.concatenate([q_ref[shard_of(tile, 0)], q_ref[shard_of(tile, 1)]], axis=0)

    def scores(queries, keys):
        return lax.dot_general(queries, keys, (((1,), (1,)), ((), ())), preferred_element_type=F32)

    def fold_max(block, running):
        for n in range(block.shape[1] // HD):
            running = jnp.maximum(running, block[:, n * HD : (n + 1) * HD])
        return running

    def score_block(tile, queries, n, running):
        at = pl.multiple_of(n * KBLK, KBLK)
        block = scores(queries, kv_ref[pl.ds(at, KBLK), :HD]) + bias_ref[:, pl.ds(at, KBLK)]
        s_ref[tile % 2, :, pl.ds(at, KBLK)] = block
        return fold_max(block, running)

    def score_new(tile, queries, running):
        block = scores(queries, new_ref[:, :HD])
        place = lax.broadcasted_iota(jnp.int32, (TILE, BLOCK), 0)
        row = place % SHARD + SHARD * jnp.where(place < TILE // 2, shard_of(tile, 0), shard_of(tile, 1))
        column = lax.broadcasted_iota(jnp.int32, (TILE, BLOCK), 1)
        block = jnp.where(column <= row, block, MASKED)
        s_ref[tile % 2, :, PREFIX:] = block
        return fold_max(block, running)

    def weigh(tile, at, width, row_max, values, total, sums):
        e = jnp.exp2((s_ref[tile % 2, :, pl.ds(at, width)] - row_max) * EXP_SCALE)
        for n in range(width // HD):
            total = total + e[:, n * HD : (n + 1) * HD]
        return total, sums + jnp.dot(e.astype(BF16), values, preferred_element_type=F32)

    lowest = jnp.full((TILE, HD), MASKED, F32)
    zeros = jnp.zeros((TILE, HD), F32)
    per = KBLK and CHROWS // KBLK
    running = lowest
    queries = query_tile(0)
    for n in range(NKB):
        if n % per == 0:
            cache_copy(n // per, pool_hbm.at[pl.ds((n // per) * CHROWS, CHROWS)]).wait()
        running = score_block(0, queries, n, running)
    running = score_new(0, queries, running)
    for tile in range(tiles):
        row_max = jnp.max(running, axis=1, keepdims=True)
        last = tile == tiles - 1
        queries = None if last else query_tile(tile + 1)

        def step(n, carry):
            running, total, sums = carry
            at = pl.multiple_of(n * KBLK, KBLK)
            if not last:
                running = score_block(tile + 1, queries, n, running)
            total, sums = weigh(tile, at, KBLK, row_max, kv_ref[pl.ds(at, KBLK), HD:], total, sums)
            return running, total, sums

        running, total, sums = lax.fori_loop(0, NKB, step, (lowest, zeros, zeros))
        if not last:
            running = score_new(tile + 1, queries, running)
        total, sums = weigh(tile, PREFIX, BLOCK, row_max, new_ref[:, HD:], total, sums)
        attended = (sums / jnp.sum(total, axis=1, keepdims=True)).astype(BF16)
        for half in range(2):
            for n in range(HEADS):
                at = half * HEADS * SHARD + n * SHARD
                to = (2 * tile + half) * SHARD
                att_ref[to : to + SHARD, n * HD : (n + 1) * HD] = attended[at : at + SHARD, :]
    wo_copy.wait()
    out_ref[...] = jnp.dot(att_ref[...], wo_ref[...], preferred_element_type=F32).astype(BF16)


def attend(info, picks, queries, new_kv, bias, w_output, pool, handed):
    tiles = len(picks) // 2
    rows = len(picks) * SHARD
    width = w_output.shape[1]
    return pl.pallas_call(
        functools.partial(attention_kernel, tiles, picks),
        out_shape=jax.ShapeDtypeStruct((rows, width), BF16),
        in_specs=[SMEM, VMEM, VMEM, VMEM, ANY, ANY] + [ANY] * NCH,
        out_specs=VMEM,
        scratch_shapes=[
            pltpu.VMEM((PREFIX, 2 * HD), BF16),
            pltpu.VMEM((2, TILE, KEYS), F32),
            pltpu.VMEM((rows, HEADS * HD), BF16),
            pltpu.VMEM(w_output.shape, BF16),
            pltpu.SemaphoreType.DMA((NCH,)),
            pltpu.SemaphoreType.DMA,
        ],
        compiler_params=pltpu.CompilerParams(vmem_limit_bytes=48 * MIB),
        cost_estimate=pl.CostEstimate(
            flops=4 * tiles * TILE * KEYS * HD, bytes_accessed=9 * 10**6, transcendentals=tiles * TILE * KEYS
        ),
        name="attend",
    )(info, queries, new_kv, bias, w_output, pool, *handed)


def pick_kernel(source_ref, pages_hbm, out_hbm, sem):
    count = out_hbm.shape[0]

    def copy(k, source):
        return pltpu.make_async_copy(pages_hbm.at[source], out_hbm.at[k], sem)

    for k in range(count):
        copy(k, source_ref[k]).start()
    pltpu.make_async_copy(pages_hbm.at[pl.ds(0, count)], out_hbm, sem).wait()


def pick_pages(sources, pages, count):
    return pl.pallas_call(
        pick_kernel,
        out_shape=jax.ShapeDtypeStruct((count,) + pages.shape[1:], BF16),
        in_specs=[SMEM, ANY],
        out_specs=ANY,
        scratch_shapes=[pltpu.SemaphoreType.DMA],
        cost_estimate=pl.CostEstimate(flops=0, bytes_accessed=3 * 10**5, transcendentals=0),
        name="pick_pages",
    )(sources, pages)


def local(
    hidden,
    norm_gain,
    w_query,
    w_key,
    w_value,
    w_output,
    prefix_pool,
    page_table,
    prefix_len,
    source,
    decode_owner,
):
    groups = lax.axis_size("group")
    group = lax.axis_index("group")
    z = lax.axis_index("tensor")
    lower = (group + groups - 1) % groups
    take = source[group] == lower
    take_flag = take.astype(jnp.int32)
    count = jnp.where(take, prefix_len[lower, 1], prefix_len[group, 0])

    handed_rows = shift(hidden[0, 1], "group", 1)
    pages = prefix_pool.shape[0] // 2
    part = pages // NCH
    handed = [
        shift(prefix_pool[pages + n * part : pages + (n + 1) * part], "group", 1).reshape(CHROWS, 2 * HD)
        for n in range(NCH)
    ]
    handed_table = shift(page_table[0, 1], "group", 1)

    table = jnp.where(take, handed_table, page_table[0, 0])
    order = jnp.arange(pages, dtype=jnp.int32)
    place = jnp.sum(jnp.where(table[:, None] == order[None, :], order[:, None], 0), axis=0)
    position = place[:, None] * PAGE + jnp.arange(PAGE, dtype=jnp.int32)[None, :]
    bias = jnp.where(position < count, 0.0, MASKED).astype(F32).reshape(1, PREFIX)

    positions = (count + jnp.arange(BLOCK, dtype=jnp.int32)).astype(F32)
    frequency = THETA ** (-(jnp.arange(HD // 2, dtype=F32) * 2.0) / HD)
    angles = positions[:, None] * frequency
    cosine = jnp.cos(angles)
    sine = jnp.sin(angles)
    cosine = jnp.concatenate([cosine, cosine], axis=1)
    sine = jnp.concatenate([-sine, sine], axis=1)

    rows, normed = choose_and_norm(take_flag[None], hidden[0, 0], handed_rows, norm_gain[None])

    up, down = [normed], [normed]
    for _ in range(NT // 2 - 1):
        up.append(shift(up[-1], "tensor", 1))
        down.append(shift(down[-1], "tensor", -1))
    half = SHARD // 2
    opposite = jnp.concatenate([shift(up[-1][:half], "tensor", 1), shift(down[-1][half:], "tensor", -1)], axis=0)
    shards = down + [opposite] + up[:0:-1]
    queries, new_kv = project(z[None], shards, cosine, sine, w_query, w_key, w_value)

    page_count = BLOCK // PAGE
    everywhere = lax.all_gather(new_kv.reshape(page_count, PAGE, 2 * HD), "group", axis=0, tiled=True)
    sender = jnp.argmax(decode_owner == group, axis=0).astype(jnp.int32)
    kv_pool = pick_pages(sender * page_count + jnp.arange(page_count, dtype=jnp.int32), everywhere, page_count)

    info = jnp.stack([z.astype(jnp.int32), take_flag])
    pool = prefix_pool.reshape(2 * PREFIX, 2 * HD)
    first = attend(info, (4, 3, 5, 2), queries, new_kv, bias, w_output, pool, handed)
    second = attend(info, (6, 1, 7, 0), queries, new_kv, bias, w_output, pool, handed)
    parts = {}
    for n, pick in enumerate((4, 3, 5, 2)):
        parts[pick] = first[n * SHARD : (n + 1) * SHARD]
    for n, pick in enumerate((6, 1, 7, 0)):
        parts[pick] = second[n * SHARD : (n + 1) * SHARD]

    columns = w_output.shape[1] // 2
    going_up = shift(parts[4][:, :columns], "tensor", 1)
    going_down = shift(parts[4][:, columns:], "tensor", -1)

    def plus(a, b):
        return a.astype(F32) + b.astype(F32)

    next_up = jnp.concatenate(
        [plus(parts[3][:, :columns], going_up).astype(BF16), parts[3][:, columns:]], axis=1
    )
    next_down = jnp.concatenate(
        [parts[5][:, :columns], plus(parts[5][:, columns:], going_down).astype(BF16)], axis=1
    )
    for step in (2, 1):
        next_up = plus(parts[step], shift(next_up, "tensor", 1)).astype(BF16)
        next_down = plus(parts[NT - step], shift(next_down, "tensor", -1)).astype(BF16)
    branch = parts[0].astype(F32) + plus(shift(next_up, "tensor", 1), shift(next_down, "tensor", -1))
    layer_out = (rows.astype(F32) + branch).astype(BF16)
    return (layer_out, kv_pool)


def solution(mesh):
    return jax.shard_map(
        local,
        mesh=mesh,
        in_specs=(
            P("group", None, "tensor", None),
            P(),
            P(None, "tensor"),
            P(None, "tensor"),
            P(None, "tensor"),
            P("tensor", None),
            P("group", None, "tensor"),
            P("group", None, None),
            P(),
            P(),
            P(),
        ),
        out_specs=(P(("group", "tensor"), None), P("group", None, "tensor")),
        check_vma=False,
    )
```

```python
import functools
import math

import jax
import jax.numpy as jnp
from jax import lax
from jax.experimental import pallas as pl
from jax.experimental.pallas import tpu as pltpu
from jax.sharding import PartitionSpec as P

HD = 128
PAGE = 8
BLOCK = 256
PREFIX = 8192
EPS = 1e-05
THETA = 500000.0

NT = 8
HEADS = 4
SHARD = BLOCK // NT
TILE = 256
KBLK = 1024
NKB = PREFIX // KBLK
KEYS = PREFIX + BLOCK
NCH = 4
CHROWS = PREFIX // NCH
SLOTS = 2
MASKED = -1e30
EXP_SCALE = math.log2(math.e) / math.sqrt(HD)
MIB = 1 << 20
F32 = jnp.float32
BF16 = jnp.bfloat16

VMEM = pl.BlockSpec(memory_space=pltpu.VMEM)
SMEM = pl.BlockSpec(memory_space=pltpu.SMEM)
ANY = pl.BlockSpec(memory_space=pl.ANY)
HBM = pl.BlockSpec(memory_space=pltpu.HBM)


def shift(value, axis, distance):
    count = lax.axis_size(axis)
    return lax.ppermute(value, axis, [(i, (i + distance) % count) for i in range(count)])


def norm_kernel(take_ref, own_ref, handed_ref, gain_ref, rows_ref, normed_ref):
    take = take_ref[0] != 0
    rows = jnp.where(take, handed_ref[...].astype(F32), own_ref[...].astype(F32))
    rows_ref[...] = rows.astype(BF16)
    mean_square = jnp.mean(rows * rows, axis=-1, keepdims=True)
    normed_ref[...] = (rows * lax.rsqrt(mean_square + EPS) * gain_ref[...].astype(F32)).astype(BF16)


def choose_and_norm(take, own, handed, gain):
    return pl.pallas_call(
        norm_kernel,
        out_shape=[jax.ShapeDtypeStruct(own.shape, BF16)] * 2,
        in_specs=[SMEM, VMEM, VMEM, VMEM],
        out_specs=[VMEM, VMEM],
        compiler_params=pltpu.CompilerParams(vmem_limit_bytes=8 * MIB),
        cost_estimate=pl.CostEstimate(flops=10**6, bytes_accessed=10**6, transcendentals=0),
        name="choose_and_norm",
    )(take, own, handed, gain)


def qkv_kernel(z_ref, slot_ref, *refs):
    shards = refs[:NT]
    cos_ref, sin_ref, wq_hbm, wk_hbm, wv_hbm, _, q_ref, kv_ref, send_ref = refs[NT : NT + 9]
    x_ref, wq_ref, wk_ref, wv_ref, shard_sem, sems = refs[NT + 9 :]
    z = z_ref[0]
    gathers = []
    for relative, shard in enumerate(shards):
        place = lax.rem(z + relative, NT)
        to = x_ref.at[pl.ds(pl.multiple_of(place * SHARD, SHARD), SHARD)]
        gathers.append(pltpu.make_async_copy(shard, to, shard_sem.at[relative]))
    copies = [
        pltpu.make_async_copy(src, dst, sems.at[n])
        for n, (src, dst) in enumerate([(wk_hbm, wk_ref), (wv_hbm, wv_ref)])
    ]
    half = wq_hbm.shape[0] // 2
    copies += [
        pltpu.make_async_copy(wq_hbm.at[pl.ds(n * half, half)], wq_ref.at[pl.ds(n * half, half)], sems.at[2 + n])
        for n in range(2)
    ]
    for copy in gathers + copies:
        copy.start()
    cosine = cos_ref[...]
    sine = sin_ref[...]

    def rotated(values):
        return values * cosine + pltpu.roll(values, HD // 2, 1) * sine

    for copy in gathers:
        copy.wait()
    copies[0].wait()
    new_keys = rotated(jnp.dot(x_ref[...], wk_ref[...], preferred_element_type=F32))
    kv_ref[:, :HD] = new_keys.astype(BF16)
    copies[1].wait()
    new_values = jnp.dot(x_ref[...], wv_ref[...], preferred_element_type=F32)
    kv_ref[:, HD:] = new_values.astype(BF16)
    for k in range(BLOCK // PAGE):
        slot = slot_ref[k]
        send_ref[slot, :, :HD] = new_keys[k * PAGE : (k + 1) * PAGE].astype(BF16)
        send_ref[slot, :, HD:] = new_values[k * PAGE : (k + 1) * PAGE].astype(BF16)
    copies[2].wait()
    copies[3].wait()
    for pair in range(HEADS // 2):
        both = jnp.dot(x_ref[...], wq_ref[:, pair * 2 * HD : (pair + 1) * 2 * HD], preferred_element_type=F32)
        for one in range(2):
            head = rotated(both[:, one * HD : (one + 1) * HD]).astype(BF16)
            n = pair * 2 + one
            for shard in range(NT):
                q_ref[shard, n * SHARD : (n + 1) * SHARD, :] = head[shard * SHARD : (shard + 1) * SHARD, :]


def project(z, slots, count, shards, cosine, sine, w_query, w_key, w_value, bias):
    depth, query_width = w_query.shape
    return pl.pallas_call(
        qkv_kernel,
        out_shape=[
            jax.ShapeDtypeStruct((NT, HEADS * SHARD, HD), BF16),
            jax.ShapeDtypeStruct((BLOCK, 2 * HD), BF16),
            jax.ShapeDtypeStruct((count, PAGE, 2 * HD), BF16),
        ],
        in_specs=[SMEM, SMEM] + [HBM] * NT + [VMEM] * 2 + [HBM] * 3 + [ANY],
        out_specs=[VMEM, VMEM, VMEM],
        scratch_shapes=[
            pltpu.VMEM((BLOCK, depth), BF16),
            pltpu.VMEM(w_query.shape, BF16),
            pltpu.VMEM(w_key.shape, BF16),
            pltpu.VMEM(w_value.shape, BF16),
            pltpu.SemaphoreType.DMA((NT,)),
            pltpu.SemaphoreType.DMA((4,)),
        ],
        compiler_params=pltpu.CompilerParams(vmem_limit_bytes=60 * MIB),
        cost_estimate=pl.CostEstimate(
            flops=2 * BLOCK * depth * (query_width + 2 * HD), bytes_accessed=9 * 10**6, transcendentals=0
        ),
        name="project",
    )(z, slots, *shards, cosine, sine, w_query, w_key, w_value, bias)


def attention_kernel(picks, info_ref, q_ref, new_ref, bias_ref, wo_hbm, pool_hbm, handed_hbm, *refs):
    out_ref, kv_ref, s_ref, att_ref, wo_ref, kv_sem, wo_sem = refs[-7:]
    z = info_ref[0]
    take = info_ref[1]

    def cache_copy(n, source):
        part = pl.ds(n * CHROWS, CHROWS)
        return pltpu.make_async_copy(source.at[part], kv_ref.at[part], kv_sem.at[n])

    @pl.when(take != 0)
    def _():
        for n in range(NCH):
            cache_copy(n, handed_hbm).start()

    @pl.when(take == 0)
    def _():
        for n in range(NCH):
            cache_copy(n, pool_hbm).start()

    wo_copy = pltpu.make_async_copy(wo_hbm, wo_ref, wo_sem)
    wo_copy.start()
    places = [lax.rem(z + pick, NT) for pick in picks]
    queries = jnp.concatenate([q_ref[place] for place in places], axis=0)

    def scores(keys):
        return lax.dot_general(queries, keys, (((1,), (1,)), ((), ())), preferred_element_type=F32)

    def fold_max(block, running):
        for n in range(block.shape[1] // HD):
            running = jnp.maximum(running, block[:, n * HD : (n + 1) * HD])
        return running

    def weigh(at, width, row_max, values, total, sums):
        e = jnp.exp2((s_ref[:, at : at + width] - row_max) * EXP_SCALE)
        for n in range(width // HD):
            total = total + e[:, n * HD : (n + 1) * HD]
        return total, sums + jnp.dot(e.astype(BF16), values, preferred_element_type=F32)

    running = jnp.full((TILE, HD), MASKED, F32)
    block = scores(new_ref[:, :HD])
    place = lax.broadcasted_iota(jnp.int32, (TILE, BLOCK), 0)
    row = place % SHARD + SHARD * jnp.where(place < TILE // 2, places[0], places[1])
    column = lax.broadcasted_iota(jnp.int32, (TILE, BLOCK), 1)
    block = jnp.where(column <= row, block, MASKED)
    s_ref[:, PREFIX:] = block
    running = fold_max(block, running)
    per = CHROWS // KBLK
    for n in range(NKB):
        if n % per == 0:
            cache_copy(n // per, pool_hbm).wait()
        at = n * KBLK
        block = scores(kv_ref[at : at + KBLK, :HD]) + bias_ref[:, at : at + KBLK]
        s_ref[:, at : at + KBLK] = block
        running = fold_max(block, running)
    row_max = jnp.max(running, axis=1, keepdims=True)
    zeros = jnp.zeros((TILE, HD), F32)
    total, sums = weigh(PREFIX, BLOCK, row_max, new_ref[:, HD:], zeros, zeros)
    for n in range(NKB):
        at = n * KBLK
        total, sums = weigh(at, KBLK, row_max, kv_ref[at : at + KBLK, HD:], total, sums)
    attended = (sums / jnp.sum(total, axis=1, keepdims=True)).astype(BF16)
    for half in range(2):
        for n in range(HEADS):
            at = half * HEADS * SHARD + n * SHARD
            to = half * SHARD
            att_ref[to : to + SHARD, n * HD : (n + 1) * HD] = attended[at : at + SHARD, :]
    wo_copy.wait()
    out_ref[...] = jnp.dot(att_ref[...], wo_ref[...], preferred_element_type=F32).astype(BF16)


def attend(info, picks, queries, new_kv, bias, w_output, pool, handed, *after):
    rows = len(picks) * SHARD
    width = w_output.shape[1]
    return pl.pallas_call(
        functools.partial(attention_kernel, picks),
        out_shape=jax.ShapeDtypeStruct((rows, width), BF16),
        in_specs=[SMEM, VMEM, VMEM, VMEM, HBM, HBM, HBM] + [ANY] * len(after),
        out_specs=VMEM,
        scratch_shapes=[
            pltpu.VMEM((PREFIX, 2 * HD), BF16),
            pltpu.VMEM((TILE, KEYS), F32),
            pltpu.VMEM((rows, HEADS * HD), BF16),
            pltpu.VMEM(w_output.shape, BF16),
            pltpu.SemaphoreType.DMA((NCH,)),
            pltpu.SemaphoreType.DMA,
        ],
        compiler_params=pltpu.CompilerParams(vmem_limit_bytes=60 * MIB),
        cost_estimate=pl.CostEstimate(
            flops=8 * TILE * KEYS * HD, bytes_accessed=9 * 10**6, transcendentals=TILE * KEYS
        ),
        name="attend",
    )(info, queries, new_kv, bias, w_output, pool, handed, *after)


def pick_kernel(source_ref, pages_ref, out_ref):
    for k in range(out_ref.shape[0]):
        out_ref[k] = pages_ref[source_ref[k]]


def pick_pages(sources, pages, count):
    return pl.pallas_call(
        pick_kernel,
        out_shape=jax.ShapeDtypeStruct((count,) + pages.shape[1:], BF16),
        in_specs=[SMEM, VMEM],
        out_specs=VMEM,
        compiler_params=pltpu.CompilerParams(vmem_limit_bytes=4 * MIB),
        cost_estimate=pl.CostEstimate(flops=0, bytes_accessed=4 * 10**5, transcendentals=0),
        name="pick_pages",
    )(sources, pages)


def local(
    hidden,
    norm_gain,
    w_query,
    w_key,
    w_value,
    w_output,
    prefix_pool,
    page_table,
    prefix_len,
    source,
    decode_owner,
):
    groups = lax.axis_size("group")
    group = lax.axis_index("group")
    z = lax.axis_index("tensor")
    lower = (group + groups - 1) % groups
    take = source[group] == lower
    take_flag = take.astype(jnp.int32)
    count = jnp.where(take, prefix_len[lower, 1], prefix_len[group, 0])

    handed_rows = shift(hidden[0, 1], "group", 1)
    pages = prefix_pool.shape[0] // 2
    handed = shift(prefix_pool[pages:], "group", 1).reshape(PREFIX, 2 * HD)
    handed_table = shift(page_table[0, 1], "group", 1)

    table = jnp.where(take, handed_table, page_table[0, 0])
    order = jnp.arange(pages, dtype=jnp.int32)
    place = jnp.sum(jnp.where(table[:, None] == order[None, :], order[:, None], 0), axis=0)
    position = place[:, None] * PAGE + jnp.arange(PAGE, dtype=jnp.int32)[None, :]
    bias = jnp.where(position < count, 0.0, MASKED).astype(F32).reshape(1, PREFIX)

    positions = (count + jnp.arange(BLOCK, dtype=jnp.int32)).astype(F32)
    frequency = THETA ** (-(jnp.arange(HD // 2, dtype=F32) * 2.0) / HD)
    angles = positions[:, None] * frequency
    cosine = jnp.cos(angles)
    sine = jnp.sin(angles)
    cosine = jnp.concatenate([cosine, cosine], axis=1)
    sine = jnp.concatenate([-sine, sine], axis=1)

    rows, normed = choose_and_norm(take_flag[None], hidden[0, 0], handed_rows, norm_gain[None])

    up, down = [normed], [normed]
    for _ in range(NT // 2 - 1):
        up.append(shift(up[-1], "tensor", 1))
        down.append(shift(down[-1], "tensor", -1))
    half = SHARD // 2
    opposite = jnp.concatenate([shift(up[-1][:half], "tensor", 1), shift(down[-1][half:], "tensor", -1)], axis=0)
    shards = down + [opposite] + up[:0:-1]

    page_count = BLOCK // PAGE
    ids = jnp.arange(page_count, dtype=jnp.int32)
    same = jnp.logical_and(decode_owner[:, :, None] == decode_owner[:, None, :], ids[None, None, :] < ids[None, :, None])
    ranks = jnp.sum(same.astype(jnp.int32), axis=-1)
    slots = decode_owner[group] * SLOTS + ranks[group]
    mine = decode_owner == group
    senders = jnp.arange(groups, dtype=jnp.int32)[:, None] * SLOTS + ranks
    sources = jnp.sum(jnp.where(mine, senders, 0), axis=0)
    queries, new_kv, outgoing = project(
        z[None], slots, groups * SLOTS, shards, cosine, sine, w_query, w_key, w_value, bias
    )
    incoming = lax.all_to_all(outgoing, "group", split_axis=0, concat_axis=0, tiled=True)
    kv_pool = pick_pages(sources, incoming, page_count)

    info = jnp.stack([z.astype(jnp.int32), take_flag])
    pool = prefix_pool.reshape(2 * PREFIX, 2 * HD)
    parts = {}
    columns = w_output.shape[1] // 2
    sent = ()
    for picks, after in (((4, 0), ()), ((3, 5), None), ((2, 6), (incoming,)), ((1, 7), ())):
        after = sent if after is None else after
        both = attend(info, picks, queries, new_kv, bias, w_output, pool, handed, *after)
        parts[picks[0]] = both[:SHARD]
        parts[picks[1]] = both[SHARD:]
        sent = sent or (parts[4][:, :columns], parts[4][:, columns:])

    going_up = shift(sent[0], "tensor", 1)
    going_down = shift(sent[1], "tensor", -1)

    def plus(a, b):
        return a.astype(F32) + b.astype(F32)

    next_up = jnp.concatenate(
        [plus(parts[3][:, :columns], going_up).astype(BF16), parts[3][:, columns:]], axis=1
    )
    next_down = jnp.concatenate(
        [parts[5][:, :columns], plus(parts[5][:, columns:], going_down).astype(BF16)], axis=1
    )
    for step in (2, 1):
        next_up = plus(parts[step], shift(next_up, "tensor", 1)).astype(BF16)
        next_down = plus(parts[NT - step], shift(next_down, "tensor", -1)).astype(BF16)
    branch = parts[0].astype(F32) + plus(shift(next_up, "tensor", 1), shift(next_down, "tensor", -1))
    layer_out = (rows.astype(F32) + branch).astype(BF16)
    return (layer_out, kv_pool)


def solution(mesh):
    return jax.shard_map(
        local,
        mesh=mesh,
        in_specs=(
            P("group", None, "tensor", None),
            P(),
            P(None, "tensor"),
            P(None, "tensor"),
            P(None, "tensor"),
            P("tensor", None),
            P("group", None, "tensor"),
            P("group", None, None),
            P(),
            P(),
            P(),
        ),
        out_specs=(P(("group", "tensor"), None), P("group", None, "tensor")),
        check_vma=False,
    )
```

```python
import functools
import math

import jax
import jax.numpy as jnp
from jax import lax
from jax.experimental import pallas as pl
from jax.experimental.pallas import tpu as pltpu
from jax.sharding import PartitionSpec as P

HD = 128
PAGE = 8
BLOCK = 256
PREFIX = 8192
EPS = 1e-05
THETA = 500000.0

NT = 8
HEADS = 4
SHARD = BLOCK // NT
TILE = 256
KBLK = 1024
NKB = PREFIX // KBLK
KEYS = PREFIX + BLOCK
NCH = 4
CHROWS = PREFIX // NCH
SLOTS = 2
MASKED = -1e30
EXP_SCALE = math.log2(math.e) / math.sqrt(HD)
MIB = 1 << 20
F32 = jnp.float32
BF16 = jnp.bfloat16

VMEM = pl.BlockSpec(memory_space=pltpu.VMEM)
SMEM = pl.BlockSpec(memory_space=pltpu.SMEM)
ANY = pl.BlockSpec(memory_space=pl.ANY)
HBM = pl.BlockSpec(memory_space=pltpu.HBM)


def shift(value, axis, distance):
    count = lax.axis_size(axis)
    return lax.ppermute(value, axis, [(i, (i + distance) % count) for i in range(count)])


def norm_kernel(take_ref, own_ref, handed_ref, gain_ref, table_ref, slot_ref, rows_ref, normed_ref, same_ref):
    take = take_ref[0] != 0
    rows = jnp.where(take, handed_ref[...].astype(F32), own_ref[...].astype(F32))
    rows_ref[...] = rows.astype(BF16)
    mean_square = jnp.mean(rows * rows, axis=-1, keepdims=True)
    normed_ref[...] = (rows * lax.rsqrt(mean_square + EPS) * gain_ref[...].astype(F32)).astype(BF16)


def choose_and_norm(take, own, handed, gain, table, slot):
    return pl.pallas_call(
        norm_kernel,
        out_shape=[jax.ShapeDtypeStruct(own.shape, BF16)] * 2 + [jax.ShapeDtypeStruct(slot.shape, BF16)],
        in_specs=[SMEM, VMEM, VMEM, VMEM, ANY, HBM],
        out_specs=[VMEM, VMEM, HBM],
        input_output_aliases={5: 2},
        compiler_params=pltpu.CompilerParams(vmem_limit_bytes=8 * MIB),
        cost_estimate=pl.CostEstimate(flops=10**6, bytes_accessed=10**6, transcendentals=0),
        name="choose_and_norm",
    )(take, own, handed, gain, table, slot)


def part_kernel(start, pool_hbm, *refs):
    out_hbm, sems = refs[-2:]
    size = out_hbm.shape[0] // NCH
    copies = []
    for n in range(NCH):
        source = pool_hbm.at[pl.ds(start + n * size, size)]
        copies.append(pltpu.make_async_copy(source, out_hbm.at[pl.ds(n * size, size)], sems.at[n]))
    for copy in copies:
        copy.start()
    for copy in copies:
        copy.wait()


def second_slot(pool, *after):
    start = pool.shape[0] // 2
    return pl.pallas_call(
        functools.partial(part_kernel, start),
        out_shape=jax.ShapeDtypeStruct((start,) + pool.shape[1:], BF16),
        in_specs=[HBM] + [ANY] * len(after),
        out_specs=HBM,
        scratch_shapes=[pltpu.SemaphoreType.DMA((NCH,))],
        cost_estimate=pl.CostEstimate(flops=0, bytes_accessed=9 * 10**6, transcendentals=0),
        name="second_slot",
    )(pool, *after)


def qkv_kernel(z_ref, slot_ref, *refs):
    shards = refs[:NT]
    cos_ref, sin_ref, wq_hbm, wk_hbm, wv_hbm, _, q_ref, kv_ref, send_ref = refs[NT : NT + 9]
    x_ref, wq_ref, wk_ref, wv_ref, shard_sem, sems = refs[NT + 9 :]
    z = z_ref[0]
    gathers = []
    for relative, shard in enumerate(shards):
        place = lax.rem(z + relative, NT)
        to = x_ref.at[pl.ds(pl.multiple_of(place * SHARD, SHARD), SHARD)]
        gathers.append(pltpu.make_async_copy(shard, to, shard_sem.at[relative]))
    copies = [
        pltpu.make_async_copy(src, dst, sems.at[n])
        for n, (src, dst) in enumerate([(wk_hbm, wk_ref), (wv_hbm, wv_ref)])
    ]
    half = wq_hbm.shape[0] // 2
    copies += [
        pltpu.make_async_copy(wq_hbm.at[pl.ds(n * half, half)], wq_ref.at[pl.ds(n * half, half)], sems.at[2 + n])
        for n in range(2)
    ]
    for copy in gathers + copies:
        copy.start()
    cosine = cos_ref[...]
    sine = sin_ref[...]

    def rotated(values):
        return values * cosine + pltpu.roll(values, HD // 2, 1) * sine

    for copy in gathers:
        copy.wait()
    copies[0].wait()
    new_keys = rotated(jnp.dot(x_ref[...], wk_ref[...], preferred_element_type=F32))
    kv_ref[:, :HD] = new_keys.astype(BF16)
    copies[1].wait()
    new_values = jnp.dot(x_ref[...], wv_ref[...], preferred_element_type=F32)
    kv_ref[:, HD:] = new_values.astype(BF16)
    for k in range(BLOCK // PAGE):
        slot = slot_ref[k]
        send_ref[slot, :, :HD] = new_keys[k * PAGE : (k + 1) * PAGE].astype(BF16)
        send_ref[slot, :, HD:] = new_values[k * PAGE : (k + 1) * PAGE].astype(BF16)
    copies[2].wait()
    copies[3].wait()
    for pair in range(HEADS // 2):
        both = jnp.dot(x_ref[...], wq_ref[:, pair * 2 * HD : (pair + 1) * 2 * HD], preferred_element_type=F32)
        for one in range(2):
            head = rotated(both[:, one * HD : (one + 1) * HD]).astype(BF16)
            n = pair * 2 + one
            for shard in range(NT):
                q_ref[shard, n * SHARD : (n + 1) * SHARD, :] = head[shard * SHARD : (shard + 1) * SHARD, :]


def project(z, slots, count, shards, cosine, sine, w_query, w_key, w_value, bias):
    depth, query_width = w_query.shape
    return pl.pallas_call(
        qkv_kernel,
        out_shape=[
            jax.ShapeDtypeStruct((NT, HEADS * SHARD, HD), BF16),
            jax.ShapeDtypeStruct((BLOCK, 2 * HD), BF16),
            jax.ShapeDtypeStruct((count, PAGE, 2 * HD), BF16),
        ],
        in_specs=[SMEM, SMEM] + [HBM] * NT + [VMEM] * 2 + [HBM] * 3 + [ANY],
        out_specs=[VMEM, VMEM, VMEM],
        scratch_shapes=[
            pltpu.VMEM((BLOCK, depth), BF16),
            pltpu.VMEM(w_query.shape, BF16),
            pltpu.VMEM(w_key.shape, BF16),
            pltpu.VMEM(w_value.shape, BF16),
            pltpu.SemaphoreType.DMA((NT,)),
            pltpu.SemaphoreType.DMA((4,)),
        ],
        compiler_params=pltpu.CompilerParams(vmem_limit_bytes=60 * MIB),
        cost_estimate=pl.CostEstimate(
            flops=2 * BLOCK * depth * (query_width + 2 * HD), bytes_accessed=9 * 10**6, transcendentals=0
        ),
        name="project",
    )(z, slots, *shards, cosine, sine, w_query, w_key, w_value, bias)


def attention_kernel(picks, info_ref, q_ref, new_ref, bias_ref, wo_hbm, pool_hbm, handed_hbm, *refs):
    out_ref, kv_ref, s_ref, att_ref, wo_ref, kv_sem, wo_sem = refs[-7:]
    z = info_ref[0]
    take = info_ref[1]

    def cache_copy(n, source):
        part = pl.ds(n * CHROWS, CHROWS)
        return pltpu.make_async_copy(source.at[part], kv_ref.at[part], kv_sem.at[n])

    @pl.when(take != 0)
    def _():
        for n in range(NCH):
            cache_copy(n, handed_hbm).start()

    @pl.when(take == 0)
    def _():
        for n in range(NCH):
            cache_copy(n, pool_hbm).start()

    wo_copy = pltpu.make_async_copy(wo_hbm, wo_ref, wo_sem)
    wo_copy.start()
    places = [lax.rem(z + pick, NT) for pick in picks]
    queries = jnp.concatenate([q_ref[place] for place in places], axis=0)

    def scores(keys):
        return lax.dot_general(queries, keys, (((1,), (1,)), ((), ())), preferred_element_type=F32)

    def fold_max(block, running):
        for n in range(block.shape[1] // HD):
            running = jnp.maximum(running, block[:, n * HD : (n + 1) * HD])
        return running

    def weigh(at, width, row_max, values, total, sums):
        e = jnp.exp2((s_ref[:, at : at + width] - row_max) * EXP_SCALE)
        for n in range(width // HD):
            total = total + e[:, n * HD : (n + 1) * HD]
        return total, sums + jnp.dot(e.astype(BF16), values, preferred_element_type=F32)

    running = jnp.full((TILE, HD), MASKED, F32)
    block = scores(new_ref[:, :HD])
    place = lax.broadcasted_iota(jnp.int32, (TILE, BLOCK), 0)
    row = place % SHARD + SHARD * jnp.where(place < TILE // 2, places[0], places[1])
    column = lax.broadcasted_iota(jnp.int32, (TILE, BLOCK), 1)
    block = jnp.where(column <= row, block, MASKED)
    s_ref[:, PREFIX:] = block
    running = fold_max(block, running)
    per = CHROWS // KBLK
    for n in range(NKB):
        if n % per == 0:
            cache_copy(n // per, pool_hbm).wait()
        at = n * KBLK
        block = scores(kv_ref[at : at + KBLK, :HD]) + bias_ref[:, at : at + KBLK]
        s_ref[:, at : at + KBLK] = block
        running = fold_max(block, running)
    row_max = jnp.max(running, axis=1, keepdims=True)
    zeros = jnp.zeros((TILE, HD), F32)
    total, sums = weigh(PREFIX, BLOCK, row_max, new_ref[:, HD:], zeros, zeros)
    for n in range(NKB):
        at = n * KBLK
        total, sums = weigh(at, KBLK, row_max, kv_ref[at : at + KBLK, HD:], total, sums)
    attended = (sums / jnp.sum(total, axis=1, keepdims=True)).astype(BF16)
    for half in range(2):
        for n in range(HEADS):
            at = half * HEADS * SHARD + n * SHARD
            to = half * SHARD
            att_ref[to : to + SHARD, n * HD : (n + 1) * HD] = attended[at : at + SHARD, :]
    wo_copy.wait()
    out_ref[...] = jnp.dot(att_ref[...], wo_ref[...], preferred_element_type=F32).astype(BF16)


def attend(info, picks, queries, new_kv, bias, w_output, pool, handed, *after):
    rows = len(picks) * SHARD
    width = w_output.shape[1]
    return pl.pallas_call(
        functools.partial(attention_kernel, picks),
        out_shape=jax.ShapeDtypeStruct((rows, width), BF16),
        in_specs=[SMEM, VMEM, VMEM, VMEM, HBM, HBM, HBM] + [ANY] * len(after),
        out_specs=VMEM,
        scratch_shapes=[
            pltpu.VMEM((PREFIX, 2 * HD), BF16),
            pltpu.VMEM((TILE, KEYS), F32),
            pltpu.VMEM((rows, HEADS * HD), BF16),
            pltpu.VMEM(w_output.shape, BF16),
            pltpu.SemaphoreType.DMA((NCH,)),
            pltpu.SemaphoreType.DMA,
        ],
        compiler_params=pltpu.CompilerParams(vmem_limit_bytes=60 * MIB),
        cost_estimate=pl.CostEstimate(
            flops=8 * TILE * KEYS * HD, bytes_accessed=9 * 10**6, transcendentals=TILE * KEYS
        ),
        name="attend",
    )(info, queries, new_kv, bias, w_output, pool, handed, *after)


def pick_kernel(source_ref, pages_ref, out_ref):
    for k in range(out_ref.shape[0]):
        out_ref[k] = pages_ref[source_ref[k]]


def pick_pages(sources, pages, count):
    return pl.pallas_call(
        pick_kernel,
        out_shape=jax.ShapeDtypeStruct((count,) + pages.shape[1:], BF16),
        in_specs=[SMEM, VMEM],
        out_specs=VMEM,
        compiler_params=pltpu.CompilerParams(vmem_limit_bytes=4 * MIB),
        cost_estimate=pl.CostEstimate(flops=0, bytes_accessed=4 * 10**5, transcendentals=0),
        name="pick_pages",
    )(sources, pages)


def local(
    hidden,
    norm_gain,
    w_query,
    w_key,
    w_value,
    w_output,
    prefix_pool,
    page_table,
    prefix_len,
    source,
    decode_owner,
):
    groups = lax.axis_size("group")
    group = lax.axis_index("group")
    z = lax.axis_index("tensor")
    lower = (group + groups - 1) % groups
    take = source[group] == lower
    take_flag = take.astype(jnp.int32)
    count = jnp.where(take, prefix_len[lower, 1], prefix_len[group, 0])

    sent_rows = hidden[0, 1]
    sent_table = page_table[0, 1]
    handed_rows = shift(sent_rows, "group", 1)
    handed_table = shift(sent_table, "group", 1)
    pages = prefix_pool.shape[0] // 2
    slot = second_slot(prefix_pool, sent_rows, sent_table)
    rows, normed, slot = choose_and_norm(
        take_flag[None], hidden[0, 0], handed_rows, norm_gain[None], handed_table[None], slot
    )
    handed = shift(slot, "group", 1).reshape(PREFIX, 2 * HD)

    table = jnp.where(take, handed_table, page_table[0, 0])
    order = jnp.arange(pages, dtype=jnp.int32)
    place = jnp.sum(jnp.where(table[:, None] == order[None, :], order[:, None], 0), axis=0)
    position = place[:, None] * PAGE + jnp.arange(PAGE, dtype=jnp.int32)[None, :]
    bias = jnp.where(position < count, 0.0, MASKED).astype(F32).reshape(1, PREFIX)

    positions = (count + jnp.arange(BLOCK, dtype=jnp.int32)).astype(F32)
    frequency = THETA ** (-(jnp.arange(HD // 2, dtype=F32) * 2.0) / HD)
    angles = positions[:, None] * frequency
    cosine = jnp.cos(angles)
    sine = jnp.sin(angles)
    cosine = jnp.concatenate([cosine, cosine], axis=1)
    sine = jnp.concatenate([-sine, sine], axis=1)

    up, down = [normed], [normed]
    for _ in range(NT // 2 - 1):
        up.append(shift(up[-1], "tensor", 1))
        down.append(shift(down[-1], "tensor", -1))
    half = SHARD // 2
    opposite = jnp.concatenate([shift(up[-1][:half], "tensor", 1), shift(down[-1][half:], "tensor", -1)], axis=0)
    shards = down + [opposite] + up[:0:-1]

    page_count = BLOCK // PAGE
    ids = jnp.arange(page_count, dtype=jnp.int32)
    same = jnp.logical_and(decode_owner[:, :, None] == decode_owner[:, None, :], ids[None, None, :] < ids[None, :, None])
    ranks = jnp.sum(same.astype(jnp.int32), axis=-1)
    slots = decode_owner[group] * SLOTS + ranks[group]
    mine = decode_owner == group
    senders = jnp.arange(groups, dtype=jnp.int32)[:, None] * SLOTS + ranks
    sources = jnp.sum(jnp.where(mine, senders, 0), axis=0)
    queries, new_kv, outgoing = project(
        z[None], slots, groups * SLOTS, shards, cosine, sine, w_query, w_key, w_value, bias
    )
    incoming = lax.all_to_all(outgoing, "group", split_axis=0, concat_axis=0, tiled=True)
    kv_pool = pick_pages(sources, incoming, page_count)

    info = jnp.stack([z.astype(jnp.int32), take_flag])
    pool = prefix_pool.reshape(2 * PREFIX, 2 * HD)
    parts = {}
    columns = w_output.shape[1] // 2
    sent = ()
    for picks, after in (((4, 0), ()), ((3, 5), None), ((2, 6), (incoming,)), ((1, 7), ())):
        after = sent if after is None else after
        both = attend(info, picks, queries, new_kv, bias, w_output, pool, handed, *after)
        parts[picks[0]] = both[:SHARD]
        parts[picks[1]] = both[SHARD:]
        sent = sent or (parts[4][:, :columns], parts[4][:, columns:])

    going_up = shift(sent[0], "tensor", 1)
    going_down = shift(sent[1], "tensor", -1)

    def plus(a, b):
        return a.astype(F32) + b.astype(F32)

    next_up = jnp.concatenate(
        [plus(parts[3][:, :columns], going_up).astype(BF16), parts[3][:, columns:]], axis=1
    )
    next_down = jnp.concatenate(
        [parts[5][:, :columns], plus(parts[5][:, columns:], going_down).astype(BF16)], axis=1
    )
    for step in (2, 1):
        next_up = plus(parts[step], shift(next_up, "tensor", 1)).astype(BF16)
        next_down = plus(parts[NT - step], shift(next_down, "tensor", -1)).astype(BF16)
    branch = parts[0].astype(F32) + plus(shift(next_up, "tensor", 1), shift(next_down, "tensor", -1))
    layer_out = (rows.astype(F32) + branch).astype(BF16)
    return (layer_out, kv_pool)


def solution(mesh):
    return jax.shard_map(
        local,
        mesh=mesh,
        in_specs=(
            P("group", None, "tensor", None),
            P(),
            P(None, "tensor"),
            P(None, "tensor"),
            P(None, "tensor"),
            P("tensor", None),
            P("group", None, "tensor"),
            P("group", None, None),
            P(),
            P(),
            P(),
        ),
        out_specs=(P(("group", "tensor"), None), P("group", None, "tensor")),
        check_vma=False,
    )
```

```python
import functools
import math

import jax
import jax.numpy as jnp
from jax import lax
from jax.experimental import pallas as pl
from jax.experimental.pallas import tpu as pltpu
from jax.sharding import PartitionSpec as P

HD = 128
PAGE = 8
BLOCK = 256
PREFIX = 8192
EPS = 1e-05
THETA = 500000.0

NT = 8
HEADS = 4
SHARD = BLOCK // NT
TILE = 256
KBLK = 512
NKB = PREFIX // KBLK
KEYS = PREFIX + BLOCK
NCH = 4
CHROWS = PREFIX // NCH
COPIES = 8
SLOTS = 2
MASKED = -1e30
EXP_SCALE = math.log2(math.e) / math.sqrt(HD)
MIB = 1 << 20
F32 = jnp.float32
BF16 = jnp.bfloat16

VMEM = pl.BlockSpec(memory_space=pltpu.VMEM)
SMEM = pl.BlockSpec(memory_space=pltpu.SMEM)
ANY = pl.BlockSpec(memory_space=pl.ANY)
HBM = pl.BlockSpec(memory_space=pltpu.HBM)


def shift(value, axis, distance):
    count = lax.axis_size(axis)
    return lax.ppermute(value, axis, [(i, (i + distance) % count) for i in range(count)])


def norm_kernel(take_ref, own_ref, handed_ref, gain_ref, table_ref, slot_ref, rows_ref, normed_ref, same_ref):
    take = take_ref[0] != 0
    rows = jnp.where(take, handed_ref[...].astype(F32), own_ref[...].astype(F32))
    rows_ref[...] = rows.astype(BF16)
    mean_square = jnp.mean(rows * rows, axis=-1, keepdims=True)
    normed_ref[...] = (rows * lax.rsqrt(mean_square + EPS) * gain_ref[...].astype(F32)).astype(BF16)


def choose_and_norm(take, own, handed, gain, table, slot):
    return pl.pallas_call(
        norm_kernel,
        out_shape=[jax.ShapeDtypeStruct(own.shape, BF16)] * 2 + [jax.ShapeDtypeStruct(slot.shape, BF16)],
        in_specs=[SMEM, VMEM, VMEM, VMEM, ANY, HBM],
        out_specs=[VMEM, VMEM, HBM],
        input_output_aliases={5: 2},
        compiler_params=pltpu.CompilerParams(vmem_limit_bytes=8 * MIB),
        cost_estimate=pl.CostEstimate(flops=10**6, bytes_accessed=10**6, transcendentals=0),
        name="choose_and_norm",
    )(take, own, handed, gain, table, slot)


def part_kernel(start, pool_hbm, *refs):
    out_hbm, stage_ref, in_sems, out_sems = refs[-4:]
    size = out_hbm.shape[0] // COPIES
    loads, stores = [], []
    for n in range(COPIES):
        part = pl.ds(n * size, size)
        source = pool_hbm.at[pl.ds(start + n * size, size)]
        loads.append(pltpu.make_async_copy(source, stage_ref.at[part], in_sems.at[n]))
        stores.append(pltpu.make_async_copy(stage_ref.at[part], out_hbm.at[part], out_sems.at[n]))
    for load in loads:
        load.start()
    for load, store in zip(loads, stores):
        load.wait()
        store.start()
    for store in stores:
        store.wait()


def second_slot(pool, *after):
    start = pool.shape[0] // 2
    shape = (start,) + pool.shape[1:]
    return pl.pallas_call(
        functools.partial(part_kernel, start),
        out_shape=jax.ShapeDtypeStruct(shape, BF16),
        in_specs=[HBM] + [ANY] * len(after),
        out_specs=HBM,
        scratch_shapes=[
            pltpu.VMEM(shape, BF16),
            pltpu.SemaphoreType.DMA((COPIES,)),
            pltpu.SemaphoreType.DMA((COPIES,)),
        ],
        compiler_params=pltpu.CompilerParams(vmem_limit_bytes=16 * MIB),
        cost_estimate=pl.CostEstimate(flops=0, bytes_accessed=9 * 10**6, transcendentals=0),
        name="second_slot",
    )(pool, *after)


def qkv_kernel(z_ref, slot_ref, *refs):
    shards = refs[:NT]
    cos_ref, sin_ref, wq_hbm, wk_hbm, wv_hbm, _, q_ref, kv_ref, send_ref = refs[NT : NT + 9]
    x_ref, wq_ref, wk_ref, wv_ref, shard_sem, sems = refs[NT + 9 :]
    z = z_ref[0]
    gathers = []
    for relative, shard in enumerate(shards):
        place = lax.rem(z + relative, NT)
        to = x_ref.at[pl.ds(pl.multiple_of(place * SHARD, SHARD), SHARD)]
        gathers.append(pltpu.make_async_copy(shard, to, shard_sem.at[relative]))
    copies = [
        pltpu.make_async_copy(src, dst, sems.at[n])
        for n, (src, dst) in enumerate([(wk_hbm, wk_ref), (wv_hbm, wv_ref)])
    ]
    half = wq_hbm.shape[0] // 2
    copies += [
        pltpu.make_async_copy(wq_hbm.at[pl.ds(n * half, half)], wq_ref.at[pl.ds(n * half, half)], sems.at[2 + n])
        for n in range(2)
    ]
    for copy in gathers + copies:
        copy.start()
    cosine = cos_ref[...]
    sine = sin_ref[...]

    def rotated(values):
        return values * cosine + pltpu.roll(values, HD // 2, 1) * sine

    for copy in gathers:
        copy.wait()
    copies[0].wait()
    new_keys = rotated(jnp.dot(x_ref[...], wk_ref[...], preferred_element_type=F32))
    kv_ref[:, :HD] = new_keys.astype(BF16)
    copies[1].wait()
    new_values = jnp.dot(x_ref[...], wv_ref[...], preferred_element_type=F32)
    kv_ref[:, HD:] = new_values.astype(BF16)
    for k in range(BLOCK // PAGE):
        slot = slot_ref[k]
        send_ref[slot, :, :HD] = new_keys[k * PAGE : (k + 1) * PAGE].astype(BF16)
        send_ref[slot, :, HD:] = new_values[k * PAGE : (k + 1) * PAGE].astype(BF16)
    copies[2].wait()
    copies[3].wait()
    for pair in range(HEADS // 2):
        both = jnp.dot(x_ref[...], wq_ref[:, pair * 2 * HD : (pair + 1) * 2 * HD], preferred_element_type=F32)
        for one in range(2):
            head = rotated(both[:, one * HD : (one + 1) * HD]).astype(BF16)
            n = pair * 2 + one
            for shard in range(NT):
                q_ref[shard, n * SHARD : (n + 1) * SHARD, :] = head[shard * SHARD : (shard + 1) * SHARD, :]


def project(z, slots, count, shards, cosine, sine, w_query, w_key, w_value, bias):
    depth, query_width = w_query.shape
    return pl.pallas_call(
        qkv_kernel,
        out_shape=[
            jax.ShapeDtypeStruct((NT, HEADS * SHARD, HD), BF16),
            jax.ShapeDtypeStruct((BLOCK, 2 * HD), BF16),
            jax.ShapeDtypeStruct((count, PAGE, 2 * HD), BF16),
        ],
        in_specs=[SMEM, SMEM] + [HBM] * NT + [VMEM] * 2 + [HBM] * 3 + [ANY],
        out_specs=[VMEM, VMEM, VMEM],
        scratch_shapes=[
            pltpu.VMEM((BLOCK, depth), BF16),
            pltpu.VMEM(w_query.shape, BF16),
            pltpu.VMEM(w_key.shape, BF16),
            pltpu.VMEM(w_value.shape, BF16),
            pltpu.SemaphoreType.DMA((NT,)),
            pltpu.SemaphoreType.DMA((4,)),
        ],
        compiler_params=pltpu.CompilerParams(vmem_limit_bytes=60 * MIB),
        cost_estimate=pl.CostEstimate(
            flops=2 * BLOCK * depth * (query_width + 2 * HD), bytes_accessed=9 * 10**6, transcendentals=0
        ),
        name="project",
    )(z, slots, *shards, cosine, sine, w_query, w_key, w_value, bias)


def attention_kernel(picks, load, info_ref, q_ref, new_ref, bias_ref, *refs):
    if load:
        wo_hbm, pool_hbm, handed_hbm, *out_refs, kv_ref, att_ref, wo_ref, wo_sem, kv_sem = refs
    else:
        wo_hbm, kv_ref, *refs = refs
        *out_refs, att_ref, wo_ref, wo_sem = refs[-5:]
    z = info_ref[0]
    take = info_ref[1]

    def cache_copy(n, source):
        part = pl.ds(n * CHROWS, CHROWS)
        return pltpu.make_async_copy(source.at[part], kv_ref.at[part], kv_sem.at[n])

    if load:

        @pl.when(take != 0)
        def _():
            for n in range(NCH):
                cache_copy(n, handed_hbm).start()

        @pl.when(take == 0)
        def _():
            for n in range(NCH):
                cache_copy(n, pool_hbm).start()

    wo_copy = pltpu.make_async_copy(wo_hbm, wo_ref, wo_sem)
    wo_copy.start()
    places = [lax.rem(z + pick, NT) for pick in picks]
    queries = jnp.concatenate([q_ref[place] for place in places], axis=0)

    def scores(keys):
        return lax.dot_general(queries, keys, (((1,), (1,)), ((), ())), preferred_element_type=F32)

    def new_scores():
        block = scores(new_ref[:, :HD])
        place = lax.broadcasted_iota(jnp.int32, (TILE, BLOCK), 0)
        row = place % SHARD + SHARD * jnp.where(place < TILE // 2, places[0], places[1])
        column = lax.broadcasted_iota(jnp.int32, (TILE, BLOCK), 1)
        return jnp.where(column <= row, block, MASKED)

    def stored_scores(n):
        if load and n % (CHROWS // KBLK) == 0:
            cache_copy(n // (CHROWS // KBLK), pool_hbm).wait()
        at = n * KBLK
        return scores(kv_ref[at : at + KBLK, :HD]) + bias_ref[:, at : at + KBLK]

    row_max = jnp.full((TILE, 1), MASKED, F32)
    total = jnp.zeros((TILE, HD), F32)
    sums = jnp.zeros((TILE, HD), F32)
    block = new_scores()
    values = new_ref[:, HD:]
    for n in range(NKB + 1):
        following = stored_scores(n) if n < NKB else None
        lanes = [slice(c * HD, (c + 1) * HD) for c in range(block.shape[1] // HD)]
        top = block[:, lanes[0]]
        for lane in lanes[1:]:
            top = jnp.maximum(top, block[:, lane])
        raised = jnp.maximum(row_max, jnp.max(top, axis=1, keepdims=True))
        keep = jnp.exp2((row_max - raised) * EXP_SCALE)
        e = jnp.exp2((block - raised) * EXP_SCALE)
        total = total * keep
        for lane in lanes:
            total = total + e[:, lane]
        sums = sums * keep + jnp.dot(e.astype(BF16), values, preferred_element_type=F32)
        row_max = raised
        block = following
        values = kv_ref[n * KBLK : (n + 1) * KBLK, HD:] if n < NKB else None
    attended = (sums / jnp.sum(total, axis=1, keepdims=True)).astype(BF16)
    for half in range(2):
        for n in range(HEADS):
            at = half * HEADS * SHARD + n * SHARD
            to = half * SHARD
            att_ref[to : to + SHARD, n * HD : (n + 1) * HD] = attended[at : at + SHARD, :]
    wo_copy.wait()
    product = jnp.dot(att_ref[...], wo_ref[...], preferred_element_type=F32).astype(BF16)
    if load:
        columns = product.shape[1] // 2
        out_refs[0][...] = product[:SHARD, :columns]
        out_refs[1][...] = product[:SHARD, columns:]
        out_refs[2][...] = product[SHARD:]
    else:
        out_refs[0][...] = product[:SHARD]
        out_refs[1][...] = product[SHARD:]


def attend(info, picks, queries, new_kv, bias, w_output, *held, after=()):
    load = len(held) == 2
    width = w_output.shape[1]
    part = lambda columns: jax.ShapeDtypeStruct((SHARD, columns), BF16)
    out_shape = [part(width // 2), part(width // 2), part(width)] if load else [part(width)] * 2
    scratch = [pltpu.VMEM((2 * SHARD, HEADS * HD), BF16), pltpu.VMEM(w_output.shape, BF16), pltpu.SemaphoreType.DMA]
    if load:
        out_shape += [jax.ShapeDtypeStruct((PREFIX, 2 * HD), BF16)]
        scratch += [pltpu.SemaphoreType.DMA((NCH,))]
    return pl.pallas_call(
        functools.partial(attention_kernel, picks, load),
        out_shape=out_shape,
        in_specs=[SMEM, VMEM, VMEM, VMEM, HBM] + ([HBM, HBM] if load else [VMEM]) + [ANY] * len(after),
        out_specs=[VMEM] * len(out_shape),
        scratch_shapes=scratch,
        compiler_params=pltpu.CompilerParams(vmem_limit_bytes=(46 if load else 24) * MIB),
        cost_estimate=pl.CostEstimate(
            flops=8 * TILE * KEYS * HD, bytes_accessed=9 * 10**6, transcendentals=TILE * KEYS
        ),
        name="attend",
    )(info, queries, new_kv, bias, w_output, *held, *after)


def plus(a, b):
    return a.astype(F32) + b.astype(F32)


def widen_kernel(up_ref, down_ref, from_left_ref, from_right_ref, up_out, down_out):
    half = from_left_ref.shape[1]
    up_out[:, :half] = plus(up_ref[:, :half], from_left_ref[...]).astype(BF16)
    up_out[:, half:] = up_ref[:, half:]
    down_out[:, :half] = down_ref[:, :half]
    down_out[:, half:] = plus(down_ref[:, half:], from_right_ref[...]).astype(BF16)


def add_kernel(up_ref, down_ref, from_left_ref, from_right_ref, up_out, down_out):
    up_out[...] = plus(up_ref[...], from_left_ref[...]).astype(BF16)
    down_out[...] = plus(down_ref[...], from_right_ref[...]).astype(BF16)


def last_kernel(rows_ref, part_ref, from_left_ref, from_right_ref, out_ref):
    branch = part_ref[...].astype(F32) + plus(from_left_ref[...], from_right_ref[...])
    out_ref[...] = (rows_ref[...].astype(F32) + branch).astype(BF16)


def combine(kernel, outputs, name, *arrays):
    shape = jax.ShapeDtypeStruct(arrays[0].shape, BF16)
    return pl.pallas_call(
        kernel,
        out_shape=[shape] * outputs,
        in_specs=[VMEM] * len(arrays),
        out_specs=[VMEM] * outputs,
        compiler_params=pltpu.CompilerParams(vmem_limit_bytes=8 * MIB),
        cost_estimate=pl.CostEstimate(flops=10**6, bytes_accessed=2 * 10**6, transcendentals=0),
        name=name,
    )(*arrays)


def pick_kernel(source_ref, pages_ref, out_ref):
    for k in range(out_ref.shape[0]):
        out_ref[k] = pages_ref[source_ref[k]]


def pick_pages(sources, pages, count):
    return pl.pallas_call(
        pick_kernel,
        out_shape=jax.ShapeDtypeStruct((count,) + pages.shape[1:], BF16),
        in_specs=[SMEM, VMEM],
        out_specs=VMEM,
        compiler_params=pltpu.CompilerParams(vmem_limit_bytes=4 * MIB),
        cost_estimate=pl.CostEstimate(flops=0, bytes_accessed=4 * 10**5, transcendentals=0),
        name="pick_pages",
    )(sources, pages)


def local(
    hidden,
    norm_gain,
    w_query,
    w_key,
    w_value,
    w_output,
    prefix_pool,
    page_table,
    prefix_len,
    source,
    decode_owner,
):
    groups = lax.axis_size("group")
    group = lax.axis_index("group")
    z = lax.axis_index("tensor")
    lower = (group + groups - 1) % groups
    take = source[group] == lower
    take_flag = take.astype(jnp.int32)
    count = jnp.where(take, prefix_len[lower, 1], prefix_len[group, 0])

    sent_rows = hidden[0, 1]
    sent_table = page_table[0, 1]
    handed_rows = shift(sent_rows, "group", 1)
    handed_table = shift(sent_table, "group", 1)
    pages = prefix_pool.shape[0] // 2
    slot = second_slot(prefix_pool, sent_rows, sent_table)
    rows, normed, slot = choose_and_norm(
        take_flag[None], hidden[0, 0], handed_rows, norm_gain[None], handed_table[None], slot
    )
    handed = shift(slot, "group", 1).reshape(PREFIX, 2 * HD)

    table = jnp.where(take, handed_table, page_table[0, 0])
    order = jnp.arange(pages, dtype=jnp.int32)
    place = jnp.sum(jnp.where(table[:, None] == order[None, :], order[:, None], 0), axis=0)
    position = place[:, None] * PAGE + jnp.arange(PAGE, dtype=jnp.int32)[None, :]
    bias = jnp.where(position < count, 0.0, MASKED).astype(F32).reshape(1, PREFIX)

    positions = (count + jnp.arange(BLOCK, dtype=jnp.int32)).astype(F32)
    frequency = THETA ** (-(jnp.arange(HD // 2, dtype=F32) * 2.0) / HD)
    angles = positions[:, None] * frequency
    cosine = jnp.cos(angles)
    sine = jnp.sin(angles)
    cosine = jnp.concatenate([cosine, cosine], axis=1)
    sine = jnp.concatenate([-sine, sine], axis=1)

    up, down = [normed], [normed]
    for _ in range(NT // 2 - 1):
        up.append(shift(up[-1], "tensor", 1))
        down.append(shift(down[-1], "tensor", -1))
    half = SHARD // 2
    opposite = jnp.concatenate([shift(up[-1][:half], "tensor", 1), shift(down[-1][half:], "tensor", -1)], axis=0)
    shards = down + [opposite] + up[:0:-1]

    page_count = BLOCK // PAGE
    ids = jnp.arange(page_count, dtype=jnp.int32)
    same = jnp.logical_and(decode_owner[:, :, None] == decode_owner[:, None, :], ids[None, None, :] < ids[None, :, None])
    ranks = jnp.sum(same.astype(jnp.int32), axis=-1)
    slots = decode_owner[group] * SLOTS + ranks[group]
    mine = decode_owner == group
    senders = jnp.arange(groups, dtype=jnp.int32)[:, None] * SLOTS + ranks
    sources = jnp.sum(jnp.where(mine, senders, 0), axis=0)
    queries, new_kv, outgoing = project(
        z[None], slots, groups * SLOTS, shards, cosine, sine, w_query, w_key, w_value, bias
    )
    incoming = lax.all_to_all(outgoing, "group", split_axis=0, concat_axis=0, tiled=True)
    kv_pool = pick_pages(sources, incoming, page_count)

    info = jnp.stack([z.astype(jnp.int32), take_flag])
    pool = prefix_pool.reshape(2 * PREFIX, 2 * HD)

    left, right, own_part, cache = attend(info, (4, 0), queries, new_kv, bias, w_output, pool, handed)
    ups, downs = {}, {}
    for distance in (3, 2, 1):
        ups[distance], downs[distance] = attend(
            info, (distance, NT - distance), queries, new_kv, bias, w_output, cache, after=(incoming,) if distance == 2 else ()
        )
    going_up, going_down = shift(left, "tensor", 1), shift(right, "tensor", -1)
    for distance in (3, 2, 1):
        kernel = widen_kernel if distance == 3 else add_kernel
        going_up, going_down = combine(kernel, 2, "add_parts", ups[distance], downs[distance], going_up, going_down)
        going_up, going_down = shift(going_up, "tensor", 1), shift(going_down, "tensor", -1)
    (layer_out,) = combine(last_kernel, 1, "add_rows", rows, own_part, going_up, going_down)
    return (layer_out, kv_pool)


def solution(mesh):
    return jax.shard_map(
        local,
        mesh=mesh,
        in_specs=(
            P("group", None, "tensor", None),
            P(),
            P(None, "tensor"),
            P(None, "tensor"),
            P(None, "tensor"),
            P("tensor", None),
            P("group", None, "tensor"),
            P("group", None, None),
            P(),
            P(),
            P(),
        ),
        out_specs=(P(("group", "tensor"), None), P("group", None, "tensor")),
        check_vma=False,
    )
```

```python
import functools
import math

import jax
import jax.numpy as jnp
from jax import lax
from jax.experimental import pallas as pl
from jax.experimental.pallas import tpu as pltpu
from jax.sharding import PartitionSpec as P

HD = 128
PAGE = 8
BLOCK = 256
PREFIX = 8192
EPS = 1e-05
THETA = 500000.0

NT = 8
HEADS = 4
SHARD = BLOCK // NT
TILE = 256
KBLK = 512
NKB = PREFIX // KBLK
KEYS = PREFIX + BLOCK
NCH = 4
CHROWS = PREFIX // NCH
COPIES = 8
SLOTS = 2
NEW_KEYS = slice(HEADS * BLOCK, (HEADS + 1) * BLOCK)
NEW_VALUES = slice((HEADS + 1) * BLOCK, (HEADS + 2) * BLOCK)
MASKED = -1e30
EXP_SCALE = math.log2(math.e) / math.sqrt(HD)
MIB = 1 << 20
F32 = jnp.float32
BF16 = jnp.bfloat16

VMEM = pl.BlockSpec(memory_space=pltpu.VMEM)
SMEM = pl.BlockSpec(memory_space=pltpu.SMEM)
ANY = pl.BlockSpec(memory_space=pl.ANY)
HBM = pl.BlockSpec(memory_space=pltpu.HBM)


def shift(value, axis, distance):
    count = lax.axis_size(axis)
    return lax.ppermute(value, axis, [(i, (i + distance) % count) for i in range(count)])


def norm_kernel(take_ref, own_ref, handed_ref, gain_ref, slot_ref, *refs):
    rows_ref, normed_ref, _ = refs[-3:]
    take = take_ref[0] != 0
    rows = jnp.where(take, handed_ref[...].astype(F32), own_ref[...].astype(F32))
    rows_ref[...] = rows.astype(BF16)
    mean_square = jnp.mean(rows * rows, axis=-1, keepdims=True)
    normed_ref[...] = (rows * lax.rsqrt(mean_square + EPS) * gain_ref[...].astype(F32)).astype(BF16)


def choose_and_norm(take, own, handed, gain, slot, *before):
    return pl.pallas_call(
        norm_kernel,
        out_shape=[jax.ShapeDtypeStruct(own.shape, BF16)] * 2 + [jax.ShapeDtypeStruct(slot.shape, BF16)],
        in_specs=[SMEM, VMEM, VMEM, VMEM, HBM] + [ANY] * len(before),
        out_specs=[VMEM, VMEM, HBM],
        input_output_aliases={4: 2},
        compiler_params=pltpu.CompilerParams(vmem_limit_bytes=8 * MIB),
        cost_estimate=pl.CostEstimate(flops=10**6, bytes_accessed=10**6, transcendentals=0),
        name="choose_and_norm",
    )(take, own, handed, gain, slot, *before)


def part_kernel(start, pool_hbm, *refs):
    out_hbm, stage_ref, in_sems, out_sems = refs[-4:]
    size = out_hbm.shape[0] // COPIES
    loads, stores = [], []
    for n in range(COPIES):
        part = pl.ds(n * size, size)
        source = pool_hbm.at[pl.ds(start + n * size, size)]
        loads.append(pltpu.make_async_copy(source, stage_ref.at[part], in_sems.at[n]))
        stores.append(pltpu.make_async_copy(stage_ref.at[part], out_hbm.at[part], out_sems.at[n]))
    for load in loads:
        load.start()
    for load, store in zip(loads, stores):
        load.wait()
        store.start()
    for store in stores:
        store.wait()


def second_slot(pool, *after):
    start = pool.shape[0] // 2
    shape = (start,) + pool.shape[1:]
    return pl.pallas_call(
        functools.partial(part_kernel, start),
        out_shape=jax.ShapeDtypeStruct(shape, BF16),
        in_specs=[HBM] + [ANY] * len(after),
        out_specs=HBM,
        scratch_shapes=[
            pltpu.VMEM(shape, BF16),
            pltpu.SemaphoreType.DMA((COPIES,)),
            pltpu.SemaphoreType.DMA((COPIES,)),
        ],
        compiler_params=pltpu.CompilerParams(vmem_limit_bytes=58 * MIB),
        cost_estimate=pl.CostEstimate(flops=0, bytes_accessed=9 * 10**6, transcendentals=0),
        name="second_slot",
    )(pool, *after)


def qkv_kernel(z_ref, slot_ref, *refs):
    shards = refs[:NT]
    cos_ref, sin_ref, wq_hbm, wk_hbm, wv_hbm, _, q_ref, send_ref = refs[NT : NT + 8]
    x_ref, wq_ref, wk_ref, wv_ref, shard_sem, sems = refs[NT + 8 :]
    z = z_ref[0]
    gathers = []
    for relative, shard in enumerate(shards):
        place = lax.rem(z + relative, NT)
        to = x_ref.at[pl.ds(pl.multiple_of(place * SHARD, SHARD), SHARD)]
        gathers.append(pltpu.make_async_copy(shard, to, shard_sem.at[relative]))
    copies = [
        pltpu.make_async_copy(src, dst, sems.at[n])
        for n, (src, dst) in enumerate([(wk_hbm, wk_ref), (wv_hbm, wv_ref)])
    ]
    half = wq_hbm.shape[0] // 2
    copies += [
        pltpu.make_async_copy(wq_hbm.at[pl.ds(n * half, half)], wq_ref.at[pl.ds(n * half, half)], sems.at[2 + n])
        for n in range(2)
    ]
    for copy in gathers + copies:
        copy.start()
    cosine = cos_ref[...]
    sine = sin_ref[...]

    def rotated(values):
        return values * cosine + pltpu.roll(values, HD // 2, 1) * sine

    for copy in gathers:
        copy.wait()
    copies[0].wait()
    new_keys = rotated(jnp.dot(x_ref[...], wk_ref[...], preferred_element_type=F32))
    q_ref[NEW_KEYS] = new_keys.astype(BF16)
    copies[1].wait()
    new_values = jnp.dot(x_ref[...], wv_ref[...], preferred_element_type=F32)
    q_ref[NEW_VALUES] = new_values.astype(BF16)
    for k in range(BLOCK // PAGE):
        slot = slot_ref[k]
        send_ref[slot, :, :HD] = new_keys[k * PAGE : (k + 1) * PAGE].astype(BF16)
        send_ref[slot, :, HD:] = new_values[k * PAGE : (k + 1) * PAGE].astype(BF16)
    copies[2].wait()
    copies[3].wait()
    for pair in range(HEADS // 2):
        both = jnp.dot(x_ref[...], wq_ref[:, pair * 2 * HD : (pair + 1) * 2 * HD], preferred_element_type=F32)
        for one in range(2):
            head = rotated(both[:, one * HD : (one + 1) * HD]).astype(BF16)
            n = pair * 2 + one
            for shard in range(NT):
                at = (shard * HEADS + n) * SHARD
                q_ref[at : at + SHARD] = head[shard * SHARD : (shard + 1) * SHARD]


def project(z, slots, count, shards, cosine, sine, w_query, w_key, w_value, bias):
    depth, query_width = w_query.shape
    return pl.pallas_call(
        qkv_kernel,
        out_shape=[
            jax.ShapeDtypeStruct(((HEADS + 2) * BLOCK, HD), BF16),
            jax.ShapeDtypeStruct((count, PAGE, 2 * HD), BF16),
        ],
        in_specs=[SMEM, SMEM] + [HBM] * NT + [VMEM] * 2 + [HBM] * 3 + [ANY],
        out_specs=[VMEM, VMEM],
        scratch_shapes=[
            pltpu.VMEM((BLOCK, depth), BF16),
            pltpu.VMEM(w_query.shape, BF16),
            pltpu.VMEM(w_key.shape, BF16),
            pltpu.VMEM(w_value.shape, BF16),
            pltpu.SemaphoreType.DMA((NT,)),
            pltpu.SemaphoreType.DMA((4,)),
        ],
        compiler_params=pltpu.CompilerParams(vmem_limit_bytes=58 * MIB),
        cost_estimate=pl.CostEstimate(
            flops=2 * BLOCK * depth * (query_width + 2 * HD), bytes_accessed=9 * 10**6, transcendentals=0
        ),
        name="project",
    )(z, slots, *shards, cosine, sine, w_query, w_key, w_value, bias)


def attention_kernel(picks, load, split, passed, info_ref, q_ref, bias_ref, *refs):
    if load:
        wo_hbm, pool_hbm, handed_hbm, *refs = refs
        kv_ref, att_ref, wo_ref, wo_sem, kv_sem = refs[-5:]
        out_refs = refs[passed : -5]
    else:
        wo_hbm, kv_ref, *refs = refs
        *out_refs, att_ref, wo_ref, wo_sem = refs[passed:]
    z = info_ref[0]
    take = info_ref[1]

    def cache_copy(n, source):
        part = pl.ds(n * CHROWS, CHROWS)
        return pltpu.make_async_copy(source.at[part], kv_ref.at[part], kv_sem.at[n])

    if load:

        @pl.when(take != 0)
        def _():
            for n in range(NCH):
                cache_copy(n, handed_hbm).start()

        @pl.when(take == 0)
        def _():
            for n in range(NCH):
                cache_copy(n, pool_hbm).start()

    wo_copy = pltpu.make_async_copy(wo_hbm, wo_ref, wo_sem)
    wo_copy.start()
    places = [lax.rem(z + pick, NT) for pick in picks]
    rows = HEADS * SHARD
    queries = jnp.concatenate([q_ref[pl.ds(pl.multiple_of(place * rows, rows), rows)] for place in places], axis=0)

    def scores(keys):
        return lax.dot_general(queries, keys, (((1,), (1,)), ((), ())), preferred_element_type=F32)

    def new_scores():
        block = scores(q_ref[NEW_KEYS])
        place = lax.broadcasted_iota(jnp.int32, (TILE, BLOCK), 0)
        row = place % SHARD + SHARD * jnp.where(place < TILE // 2, places[0], places[1])
        column = lax.broadcasted_iota(jnp.int32, (TILE, BLOCK), 1)
        return jnp.where(column <= row, block, MASKED)

    def stored_scores(n):
        if load and n % (CHROWS // KBLK) == 0:
            cache_copy(n // (CHROWS // KBLK), pool_hbm).wait()
        at = n * KBLK
        return scores(kv_ref[at : at + KBLK, :HD]) + bias_ref[:, at : at + KBLK]

    row_max = jnp.full((TILE, 1), MASKED, F32)
    total = jnp.zeros((TILE, HD), F32)
    sums = jnp.zeros((TILE, HD), F32)
    block = new_scores()
    values = q_ref[NEW_VALUES]
    for n in range(NKB + 1):
        following = stored_scores(n) if n < NKB else None
        lanes = [slice(c * HD, (c + 1) * HD) for c in range(block.shape[1] // HD)]
        top = block[:, lanes[0]]
        for lane in lanes[1:]:
            top = jnp.maximum(top, block[:, lane])
        raised = jnp.maximum(row_max, jnp.max(top, axis=1, keepdims=True))
        keep = jnp.exp2((row_max - raised) * EXP_SCALE)
        e = jnp.exp2((block - raised) * EXP_SCALE)
        total = total * keep
        for lane in lanes:
            total = total + e[:, lane]
        sums = sums * keep + jnp.dot(e.astype(BF16), values, preferred_element_type=F32)
        row_max = raised
        block = following
        values = kv_ref[n * KBLK : (n + 1) * KBLK, HD:] if n < NKB else None
    attended = (sums / jnp.sum(total, axis=1, keepdims=True)).astype(BF16)
    for half in range(2):
        for n in range(HEADS):
            at = half * HEADS * SHARD + n * SHARD
            to = half * SHARD
            att_ref[to : to + SHARD, n * HD : (n + 1) * HD] = attended[at : at + SHARD, :]
    wo_copy.wait()
    product = jnp.dot(att_ref[...], wo_ref[...], preferred_element_type=F32).astype(BF16)
    if split:
        columns = product.shape[1] // 2
        out_refs[0][...] = product[:SHARD, :columns]
        out_refs[1][...] = product[:SHARD, columns:]
        out_refs[2][...] = product[SHARD:]
    else:
        out_refs[0][...] = product[:SHARD]
        out_refs[1][...] = product[SHARD:]


def attend(info, picks, projected, bias, w_output, *held, split=False, after=()):
    load = len(held) == 2
    width = w_output.shape[1]
    part = lambda columns: jax.ShapeDtypeStruct((SHARD, columns), BF16)
    out_shape = [part(width // 2), part(width // 2), part(width)] if split else [part(width)] * 2
    scratch = [pltpu.VMEM((2 * SHARD, HEADS * HD), BF16), pltpu.VMEM(w_output.shape, BF16), pltpu.SemaphoreType.DMA]
    if load:
        scratch += [pltpu.SemaphoreType.DMA((NCH,))]
    extra = [jax.ShapeDtypeStruct((PREFIX, 2 * HD), BF16)] if load else []
    return pl.pallas_call(
        functools.partial(attention_kernel, picks, load, split, len(after)),
        out_shape=out_shape + extra,
        in_specs=[SMEM, VMEM, VMEM, HBM] + ([HBM, HBM] if load else [VMEM]) + [ANY] * len(after),
        out_specs=[VMEM] * len(out_shape + extra),
        scratch_shapes=scratch,
        compiler_params=pltpu.CompilerParams(vmem_limit_bytes=(46 if load else 24) * MIB),
        cost_estimate=pl.CostEstimate(
            flops=8 * TILE * KEYS * HD, bytes_accessed=9 * 10**6, transcendentals=TILE * KEYS
        ),
        name="attend",
    )(info, projected, bias, w_output, *held, *after)


def plus(a, b):
    return a.astype(F32) + b.astype(F32)


def widen_kernel(up_ref, down_ref, from_left_ref, from_right_ref, up_out, down_out):
    half = from_left_ref.shape[1]
    up_out[:, :half] = plus(up_ref[:, :half], from_left_ref[...]).astype(BF16)
    up_out[:, half:] = up_ref[:, half:]
    down_out[:, :half] = down_ref[:, :half]
    down_out[:, half:] = plus(down_ref[:, half:], from_right_ref[...]).astype(BF16)


def add_kernel(up_ref, down_ref, from_left_ref, from_right_ref, up_out, down_out):
    up_out[...] = plus(up_ref[...], from_left_ref[...]).astype(BF16)
    down_out[...] = plus(down_ref[...], from_right_ref[...]).astype(BF16)


def last_kernel(rows_ref, part_ref, from_left_ref, from_right_ref, out_ref):
    branch = part_ref[...].astype(F32) + plus(from_left_ref[...], from_right_ref[...])
    out_ref[...] = (rows_ref[...].astype(F32) + branch).astype(BF16)


def combine(kernel, outputs, name, *arrays):
    shape = jax.ShapeDtypeStruct(arrays[0].shape, BF16)
    return pl.pallas_call(
        kernel,
        out_shape=[shape] * outputs,
        in_specs=[VMEM] * len(arrays),
        out_specs=[VMEM] * outputs,
        compiler_params=pltpu.CompilerParams(vmem_limit_bytes=8 * MIB),
        cost_estimate=pl.CostEstimate(flops=10**6, bytes_accessed=2 * 10**6, transcendentals=0),
        name=name,
    )(*arrays)


def pick_kernel(source_ref, pages_ref, out_ref):
    for k in range(out_ref.shape[0]):
        out_ref[k] = pages_ref[source_ref[k]]


def pick_pages(sources, pages, count):
    return pl.pallas_call(
        pick_kernel,
        out_shape=jax.ShapeDtypeStruct((count,) + pages.shape[1:], BF16),
        in_specs=[SMEM, VMEM],
        out_specs=VMEM,
        compiler_params=pltpu.CompilerParams(vmem_limit_bytes=4 * MIB),
        cost_estimate=pl.CostEstimate(flops=0, bytes_accessed=4 * 10**5, transcendentals=0),
        name="pick_pages",
    )(sources, pages)


def local(
    hidden,
    norm_gain,
    w_query,
    w_key,
    w_value,
    w_output,
    prefix_pool,
    page_table,
    prefix_len,
    source,
    decode_owner,
):
    groups = lax.axis_size("group")
    group = lax.axis_index("group")
    z = lax.axis_index("tensor")
    lower = (group + groups - 1) % groups
    take = source[group] == lower
    take_flag = take.astype(jnp.int32)
    count = jnp.where(take, prefix_len[lower, 1], prefix_len[group, 0])

    sent_rows = hidden[0, 1]
    sent_table = page_table[0, 1]
    handed_rows = shift(sent_rows, "group", 1)
    handed_table = shift(sent_table, "group", 1)
    pages = prefix_pool.shape[0] // 2
    table = jnp.where(take, handed_table, page_table[0, 0])
    order = jnp.arange(pages, dtype=jnp.int32)
    place = jnp.sum(jnp.where(table[:, None] == order[None, :], order[:, None], 0), axis=0)
    position = place[:, None] * PAGE + jnp.arange(PAGE, dtype=jnp.int32)[None, :]
    bias = jnp.where(position < count, 0.0, MASKED).astype(F32).reshape(1, PREFIX)

    positions = (count + jnp.arange(BLOCK, dtype=jnp.int32)).astype(F32)
    frequency = THETA ** (-(jnp.arange(HD // 2, dtype=F32) * 2.0) / HD)
    angles = positions[:, None] * frequency
    cosine = jnp.cos(angles)
    sine = jnp.sin(angles)
    cosine = jnp.concatenate([cosine, cosine], axis=1)
    sine = jnp.concatenate([-sine, sine], axis=1)

    page_count = BLOCK // PAGE
    ids = jnp.arange(page_count, dtype=jnp.int32)
    same = jnp.logical_and(decode_owner[:, :, None] == decode_owner[:, None, :], ids[None, None, :] < ids[None, :, None])
    ranks = jnp.sum(same.astype(jnp.int32), axis=-1)
    slots = decode_owner[group] * SLOTS + ranks[group]
    mine = decode_owner == group
    senders = jnp.arange(groups, dtype=jnp.int32)[:, None] * SLOTS + ranks
    sources = jnp.sum(jnp.where(mine, senders, 0), axis=0)
    slot = second_slot(prefix_pool, sent_rows, sent_table)
    rows, normed, slot = choose_and_norm(
        take_flag[None], hidden[0, 0], handed_rows, norm_gain[None], slot, handed_table[None], cosine, sine, slots, sources
    )
    handed = shift(slot, "group", 1).reshape(PREFIX, 2 * HD)

    up, down = [normed], [normed]
    for _ in range(NT // 2 - 1):
        up.append(shift(up[-1], "tensor", 1))
        down.append(shift(down[-1], "tensor", -1))
    half = SHARD // 2
    opposite = jnp.concatenate([shift(up[-1][:half], "tensor", 1), shift(down[-1][half:], "tensor", -1)], axis=0)
    shards = down + [opposite] + up[:0:-1]

    projected, outgoing = project(
        z[None], slots, groups * SLOTS, shards, cosine, sine, w_query, w_key, w_value, bias
    )
    incoming = lax.all_to_all(outgoing, "group", split_axis=0, concat_axis=0, tiled=True)
    kv_pool = pick_pages(sources, incoming, page_count)

    info = jnp.stack([z.astype(jnp.int32), take_flag])
    pool = prefix_pool.reshape(2 * PREFIX, 2 * HD)

    work = (projected, bias, w_output)
    left, right, own_part, cache = attend(info, (4, 0), *work, pool, handed, split=True)
    ups, downs = {}, {}
    ups[3], downs[3] = attend(info, (3, 5), *work, cache)
    ups[2], downs[2], cache = attend(info, (2, 6), *work, pool, handed, after=(incoming,))
    ups[1], downs[1] = attend(info, (1, 7), *work, cache)
    going_up, going_down = shift(left, "tensor", 1), shift(right, "tensor", -1)
    for distance in (3, 2, 1):
        kernel = widen_kernel if distance == 3 else add_kernel
        going_up, going_down = combine(kernel, 2, "add_parts", ups[distance], downs[distance], going_up, going_down)
        going_up, going_down = shift(going_up, "tensor", 1), shift(going_down, "tensor", -1)
    (layer_out,) = combine(last_kernel, 1, "add_rows", rows, own_part, going_up, going_down)
    return (layer_out, kv_pool)


def solution(mesh):
    return jax.shard_map(
        local,
        mesh=mesh,
        in_specs=(
            P("group", None, "tensor", None),
            P(),
            P(None, "tensor"),
            P(None, "tensor"),
            P(None, "tensor"),
            P("tensor", None),
            P("group", None, "tensor"),
            P("group", None, None),
            P(),
            P(),
            P(),
        ),
        out_specs=(P(("group", "tensor"), None), P("group", None, "tensor")),
        check_vma=False,
    )
```

```python
import functools
import math

import jax
import jax.numpy as jnp
from jax import lax
from jax.experimental import pallas as pl
from jax.experimental.pallas import tpu as pltpu
from jax.sharding import PartitionSpec as P

HD = 128
PAGE = 8
BLOCK = 256
PREFIX = 8192
EPS = 1e-05
THETA = 500000.0

NT = 8
HEADS = 4
SHARD = BLOCK // NT
TILE = 256
KBLK = 512
NKB = PREFIX // KBLK
KEYS = PREFIX + BLOCK
NCH = 4
CHROWS = PREFIX // NCH
COPIES = 8
SLOTS = 2
NEW_KEYS = slice(HEADS * BLOCK, (HEADS + 1) * BLOCK)
NEW_VALUES = slice((HEADS + 1) * BLOCK, (HEADS + 2) * BLOCK)
MASKED = -1e30
EXP_SCALE = math.log2(math.e) / math.sqrt(HD)
MIB = 1 << 20
F32 = jnp.float32
BF16 = jnp.bfloat16

VMEM = pl.BlockSpec(memory_space=pltpu.VMEM)
SMEM = pl.BlockSpec(memory_space=pltpu.SMEM)
ANY = pl.BlockSpec(memory_space=pl.ANY)
HBM = pl.BlockSpec(memory_space=pltpu.HBM)


def shift(value, axis, distance):
    count = lax.axis_size(axis)
    return lax.ppermute(value, axis, [(i, (i + distance) % count) for i in range(count)])


def norm_kernel(take_ref, own_ref, handed_ref, gain_ref, slot_ref, *refs):
    rows_ref, normed_ref, _ = refs[-3:]
    take = take_ref[0] != 0
    rows = jnp.where(take, handed_ref[...].astype(F32), own_ref[...].astype(F32))
    rows_ref[...] = rows.astype(BF16)
    mean_square = jnp.mean(rows * rows, axis=-1, keepdims=True)
    normed_ref[...] = (rows * lax.rsqrt(mean_square + EPS) * gain_ref[...].astype(F32)).astype(BF16)


def choose_and_norm(take, own, handed, gain, slot, *before):
    return pl.pallas_call(
        norm_kernel,
        out_shape=[jax.ShapeDtypeStruct(own.shape, BF16)] * 2 + [jax.ShapeDtypeStruct(slot.shape, BF16)],
        in_specs=[SMEM, VMEM, VMEM, VMEM, HBM] + [ANY] * len(before),
        out_specs=[VMEM, VMEM, HBM],
        input_output_aliases={4: 2},
        compiler_params=pltpu.CompilerParams(vmem_limit_bytes=8 * MIB),
        cost_estimate=pl.CostEstimate(flops=10**6, bytes_accessed=10**6, transcendentals=0),
        name="choose_and_norm",
    )(take, own, handed, gain, slot, *before)


def later_kernel(count, *refs):
    for source_ref, out_ref in zip(refs[:count], refs[-count:]):
        out_ref[...] = source_ref[...]


def later(arrays, *before):
    return pl.pallas_call(
        functools.partial(later_kernel, len(arrays)),
        out_shape=[jax.ShapeDtypeStruct(x.shape, x.dtype) for x in arrays],
        in_specs=[VMEM] * len(arrays) + [ANY] * len(before),
        out_specs=[VMEM] * len(arrays),
        compiler_params=pltpu.CompilerParams(vmem_limit_bytes=4 * MIB),
        cost_estimate=pl.CostEstimate(flops=0, bytes_accessed=10**4, transcendentals=0),
        name="later",
    )(*arrays, *before)


def part_kernel(start, pool_hbm, *refs):
    out_hbm, stage_ref, in_sems, out_sems = refs[-4:]
    size = out_hbm.shape[0] // COPIES
    loads, stores = [], []
    for n in range(COPIES):
        part = pl.ds(n * size, size)
        source = pool_hbm.at[pl.ds(start + n * size, size)]
        loads.append(pltpu.make_async_copy(source, stage_ref.at[part], in_sems.at[n]))
        stores.append(pltpu.make_async_copy(stage_ref.at[part], out_hbm.at[part], out_sems.at[n]))
    for load in loads:
        load.start()
    for load, store in zip(loads, stores):
        load.wait()
        store.start()
    for store in stores:
        store.wait()


def second_slot(pool, *after):
    start = pool.shape[0] // 2
    shape = (start,) + pool.shape[1:]
    return pl.pallas_call(
        functools.partial(part_kernel, start),
        out_shape=jax.ShapeDtypeStruct(shape, BF16),
        in_specs=[HBM] + [ANY] * len(after),
        out_specs=HBM,
        scratch_shapes=[
            pltpu.VMEM(shape, BF16),
            pltpu.SemaphoreType.DMA((COPIES,)),
            pltpu.SemaphoreType.DMA((COPIES,)),
        ],
        compiler_params=pltpu.CompilerParams(vmem_limit_bytes=58 * MIB),
        cost_estimate=pl.CostEstimate(flops=0, bytes_accessed=9 * 10**6, transcendentals=0),
        name="second_slot",
    )(pool, *after)


def qkv_kernel(z_ref, slot_ref, *refs):
    shards = refs[:NT]
    cos_ref, sin_ref, wq_hbm, wk_hbm, wv_hbm, _, q_ref, send_ref = refs[NT : NT + 8]
    x_ref, wq_ref, wk_ref, wv_ref, shard_sem, sems = refs[NT + 8 :]
    z = z_ref[0]
    gathers = []
    for relative, shard in enumerate(shards):
        place = lax.rem(z + relative, NT)
        to = x_ref.at[pl.ds(pl.multiple_of(place * SHARD, SHARD), SHARD)]
        gathers.append(pltpu.make_async_copy(shard, to, shard_sem.at[relative]))
    copies = [
        pltpu.make_async_copy(src, dst, sems.at[n])
        for n, (src, dst) in enumerate([(wk_hbm, wk_ref), (wv_hbm, wv_ref)])
    ]
    half = wq_hbm.shape[0] // 2
    copies += [
        pltpu.make_async_copy(wq_hbm.at[pl.ds(n * half, half)], wq_ref.at[pl.ds(n * half, half)], sems.at[2 + n])
        for n in range(2)
    ]
    for copy in gathers + copies:
        copy.start()
    cosine = cos_ref[...]
    sine = sin_ref[...]

    def rotated(values):
        return values * cosine + pltpu.roll(values, HD // 2, 1) * sine

    for copy in gathers:
        copy.wait()
    copies[0].wait()
    new_keys = rotated(jnp.dot(x_ref[...], wk_ref[...], preferred_element_type=F32))
    q_ref[NEW_KEYS] = new_keys.astype(BF16)
    copies[1].wait()
    new_values = jnp.dot(x_ref[...], wv_ref[...], preferred_element_type=F32)
    q_ref[NEW_VALUES] = new_values.astype(BF16)
    for k in range(BLOCK // PAGE):
        slot = slot_ref[k]
        send_ref[slot, :, :HD] = new_keys[k * PAGE : (k + 1) * PAGE].astype(BF16)
        send_ref[slot, :, HD:] = new_values[k * PAGE : (k + 1) * PAGE].astype(BF16)
    copies[2].wait()
    copies[3].wait()
    for pair in range(HEADS // 2):
        both = jnp.dot(x_ref[...], wq_ref[:, pair * 2 * HD : (pair + 1) * 2 * HD], preferred_element_type=F32)
        for one in range(2):
            head = rotated(both[:, one * HD : (one + 1) * HD]).astype(BF16)
            n = pair * 2 + one
            for shard in range(NT):
                at = (shard * HEADS + n) * SHARD
                q_ref[at : at + SHARD] = head[shard * SHARD : (shard + 1) * SHARD]


def project(z, slots, count, shards, cosine, sine, w_query, w_key, w_value, bias):
    depth, query_width = w_query.shape
    return pl.pallas_call(
        qkv_kernel,
        out_shape=[
            jax.ShapeDtypeStruct(((HEADS + 2) * BLOCK, HD), BF16),
            jax.ShapeDtypeStruct((count, PAGE, 2 * HD), BF16),
        ],
        in_specs=[SMEM, SMEM] + [HBM] * NT + [VMEM] * 2 + [HBM] * 3 + [ANY],
        out_specs=[VMEM, VMEM],
        scratch_shapes=[
            pltpu.VMEM((BLOCK, depth), BF16),
            pltpu.VMEM(w_query.shape, BF16),
            pltpu.VMEM(w_key.shape, BF16),
            pltpu.VMEM(w_value.shape, BF16),
            pltpu.SemaphoreType.DMA((NT,)),
            pltpu.SemaphoreType.DMA((4,)),
        ],
        compiler_params=pltpu.CompilerParams(vmem_limit_bytes=58 * MIB),
        cost_estimate=pl.CostEstimate(
            flops=2 * BLOCK * depth * (query_width + 2 * HD), bytes_accessed=9 * 10**6, transcendentals=0
        ),
        name="project",
    )(z, slots, *shards, cosine, sine, w_query, w_key, w_value, bias)


def attention_kernel(picks, load, split, passed, info_ref, q_ref, bias_ref, *refs):
    if load:
        wo_hbm, pool_hbm, handed_hbm, *refs = refs
        kv_ref, att_ref, wo_ref, wo_sem, kv_sem = refs[-5:]
        out_refs = refs[passed : -5]
    else:
        wo_hbm, kv_ref, *refs = refs
        *out_refs, att_ref, wo_ref, wo_sem = refs[passed:]
    z = info_ref[0]
    take = info_ref[1]

    def cache_copy(n, source):
        part = pl.ds(n * CHROWS, CHROWS)
        return pltpu.make_async_copy(source.at[part], kv_ref.at[part], kv_sem.at[n])

    if load:

        @pl.when(take != 0)
        def _():
            for n in range(NCH):
                cache_copy(n, handed_hbm).start()

        @pl.when(take == 0)
        def _():
            for n in range(NCH):
                cache_copy(n, pool_hbm).start()

    wo_copy = pltpu.make_async_copy(wo_hbm, wo_ref, wo_sem)
    wo_copy.start()
    places = [lax.rem(z + pick, NT) for pick in picks]
    rows = HEADS * SHARD
    queries = jnp.concatenate([q_ref[pl.ds(pl.multiple_of(place * rows, rows), rows)] for place in places], axis=0)

    def scores(keys):
        return lax.dot_general(queries, keys, (((1,), (1,)), ((), ())), preferred_element_type=F32)

    def new_scores():
        block = scores(q_ref[NEW_KEYS])
        place = lax.broadcasted_iota(jnp.int32, (TILE, BLOCK), 0)
        row = place % SHARD + SHARD * jnp.where(place < TILE // 2, places[0], places[1])
        column = lax.broadcasted_iota(jnp.int32, (TILE, BLOCK), 1)
        return jnp.where(column <= row, block, MASKED)

    def stored_scores(n):
        if load and n % (CHROWS // KBLK) == 0:
            cache_copy(n // (CHROWS // KBLK), pool_hbm).wait()
        at = n * KBLK
        return scores(kv_ref[at : at + KBLK, :HD]) + bias_ref[:, at : at + KBLK]

    row_max = jnp.full((TILE, 1), MASKED, F32)
    total = jnp.zeros((TILE, HD), F32)
    sums = jnp.zeros((TILE, HD), F32)
    block = new_scores()
    values = q_ref[NEW_VALUES]
    for n in range(NKB + 1):
        following = stored_scores(n) if n < NKB else None
        lanes = [slice(c * HD, (c + 1) * HD) for c in range(block.shape[1] // HD)]
        top = block[:, lanes[0]]
        for lane in lanes[1:]:
            top = jnp.maximum(top, block[:, lane])
        raised = jnp.maximum(row_max, jnp.max(top, axis=1, keepdims=True))
        keep = jnp.exp2((row_max - raised) * EXP_SCALE)
        e = jnp.exp2((block - raised) * EXP_SCALE)
        total = total * keep
        for lane in lanes:
            total = total + e[:, lane]
        sums = sums * keep + jnp.dot(e.astype(BF16), values, preferred_element_type=F32)
        row_max = raised
        block = following
        values = kv_ref[n * KBLK : (n + 1) * KBLK, HD:] if n < NKB else None
    attended = (sums / jnp.sum(total, axis=1, keepdims=True)).astype(BF16)
    for half in range(2):
        for n in range(HEADS):
            at = half * HEADS * SHARD + n * SHARD
            to = half * SHARD
            att_ref[to : to + SHARD, n * HD : (n + 1) * HD] = attended[at : at + SHARD, :]
    wo_copy.wait()
    product = jnp.dot(att_ref[...], wo_ref[...], preferred_element_type=F32).astype(BF16)
    if split:
        columns = product.shape[1] // 2
        out_refs[0][...] = product[:SHARD, :columns]
        out_refs[1][...] = product[:SHARD, columns:]
        out_refs[2][...] = product[SHARD:]
    else:
        out_refs[0][...] = product[:SHARD]
        out_refs[1][...] = product[SHARD:]


def attend(info, picks, projected, bias, w_output, *held, split=False, after=()):
    load = len(held) == 2
    width = w_output.shape[1]
    part = lambda columns: jax.ShapeDtypeStruct((SHARD, columns), BF16)
    out_shape = [part(width // 2), part(width // 2), part(width)] if split else [part(width)] * 2
    scratch = [pltpu.VMEM((2 * SHARD, HEADS * HD), BF16), pltpu.VMEM(w_output.shape, BF16), pltpu.SemaphoreType.DMA]
    if load:
        scratch += [pltpu.SemaphoreType.DMA((NCH,))]
    extra = [jax.ShapeDtypeStruct((PREFIX, 2 * HD), BF16)] if load else []
    return pl.pallas_call(
        functools.partial(attention_kernel, picks, load, split, len(after)),
        out_shape=out_shape + extra,
        in_specs=[SMEM, VMEM, VMEM, HBM] + ([HBM, HBM] if load else [VMEM]) + [ANY] * len(after),
        out_specs=[VMEM] * len(out_shape + extra),
        scratch_shapes=scratch,
        compiler_params=pltpu.CompilerParams(vmem_limit_bytes=(46 if load else 24) * MIB),
        cost_estimate=pl.CostEstimate(
            flops=8 * TILE * KEYS * HD, bytes_accessed=9 * 10**6, transcendentals=TILE * KEYS
        ),
        name="attend",
    )(info, projected, bias, w_output, *held, *after)


def plus(a, b):
    return a.astype(F32) + b.astype(F32)


def widen_kernel(up_ref, down_ref, from_left_ref, from_right_ref, up_out, down_out):
    half = from_left_ref.shape[1]
    up_out[:, :half] = plus(up_ref[:, :half], from_left_ref[...]).astype(BF16)
    up_out[:, half:] = up_ref[:, half:]
    down_out[:, :half] = down_ref[:, :half]
    down_out[:, half:] = plus(down_ref[:, half:], from_right_ref[...]).astype(BF16)


def add_kernel(up_ref, down_ref, from_left_ref, from_right_ref, up_out, down_out):
    up_out[...] = plus(up_ref[...], from_left_ref[...]).astype(BF16)
    down_out[...] = plus(down_ref[...], from_right_ref[...]).astype(BF16)


def last_kernel(rows_ref, part_ref, from_left_ref, from_right_ref, out_ref):
    branch = part_ref[...].astype(F32) + plus(from_left_ref[...], from_right_ref[...])
    out_ref[...] = (rows_ref[...].astype(F32) + branch).astype(BF16)


def combine(kernel, outputs, name, *arrays):
    shape = jax.ShapeDtypeStruct(arrays[0].shape, BF16)
    return pl.pallas_call(
        kernel,
        out_shape=[shape] * outputs,
        in_specs=[VMEM] * len(arrays),
        out_specs=[VMEM] * outputs,
        compiler_params=pltpu.CompilerParams(vmem_limit_bytes=8 * MIB),
        cost_estimate=pl.CostEstimate(flops=10**6, bytes_accessed=2 * 10**6, transcendentals=0),
        name=name,
    )(*arrays)


def pick_kernel(source_ref, pages_ref, out_ref):
    for k in range(out_ref.shape[0]):
        out_ref[k] = pages_ref[source_ref[k]]


def pick_pages(sources, pages, count):
    return pl.pallas_call(
        pick_kernel,
        out_shape=jax.ShapeDtypeStruct((count,) + pages.shape[1:], BF16),
        in_specs=[SMEM, VMEM],
        out_specs=VMEM,
        compiler_params=pltpu.CompilerParams(vmem_limit_bytes=4 * MIB),
        cost_estimate=pl.CostEstimate(flops=0, bytes_accessed=4 * 10**5, transcendentals=0),
        name="pick_pages",
    )(sources, pages)


def local(
    hidden,
    norm_gain,
    w_query,
    w_key,
    w_value,
    w_output,
    prefix_pool,
    page_table,
    prefix_len,
    source,
    decode_owner,
):
    groups = lax.axis_size("group")
    group = lax.axis_index("group")
    z = lax.axis_index("tensor")
    lower = (group + groups - 1) % groups
    take = source[group] == lower
    take_flag = take.astype(jnp.int32)

    sent_rows = hidden[0, 1]
    sent_table = page_table[0, 1]
    handed_rows = shift(sent_rows, "group", 1)
    handed_table = shift(sent_table, "group", 1)
    pages = prefix_pool.shape[0] // 2
    slot = second_slot(prefix_pool, sent_rows, sent_table)
    rows, normed, slot = choose_and_norm(
        take_flag[None], hidden[0, 0], handed_rows, norm_gain[None], slot, handed_table[None]
    )
    handed = shift(slot, "group", 1).reshape(PREFIX, 2 * HD)

    up, down = [normed], [normed]
    for _ in range(NT // 2 - 1):
        up.append(shift(up[-1], "tensor", 1))
        down.append(shift(down[-1], "tensor", -1))
    prefix_len, decode_owner, handed_table = later((prefix_len, decode_owner, handed_table[None]), up[1])
    count = jnp.where(take, prefix_len[lower, 1], prefix_len[group, 0])
    half = SHARD // 2
    opposite = jnp.concatenate([shift(up[-1][:half], "tensor", 1), shift(down[-1][half:], "tensor", -1)], axis=0)
    shards = down + [opposite] + up[:0:-1]

    table = jnp.where(take, handed_table[0], page_table[0, 0])
    order = jnp.arange(pages, dtype=jnp.int32)
    place = jnp.sum(jnp.where(table[:, None] == order[None, :], order[:, None], 0), axis=0)
    position = place[:, None] * PAGE + jnp.arange(PAGE, dtype=jnp.int32)[None, :]
    bias = jnp.where(position < count, 0.0, MASKED).astype(F32).reshape(1, PREFIX)

    positions = (count + jnp.arange(BLOCK, dtype=jnp.int32)).astype(F32)
    frequency = THETA ** (-(jnp.arange(HD // 2, dtype=F32) * 2.0) / HD)
    angles = positions[:, None] * frequency
    cosine = jnp.cos(angles)
    sine = jnp.sin(angles)
    cosine = jnp.concatenate([cosine, cosine], axis=1)
    sine = jnp.concatenate([-sine, sine], axis=1)

    page_count = BLOCK // PAGE
    ids = jnp.arange(page_count, dtype=jnp.int32)
    same = jnp.logical_and(decode_owner[:, :, None] == decode_owner[:, None, :], ids[None, None, :] < ids[None, :, None])
    ranks = jnp.sum(same.astype(jnp.int32), axis=-1)
    slots = decode_owner[group] * SLOTS + ranks[group]
    mine = decode_owner == group
    senders = jnp.arange(groups, dtype=jnp.int32)[:, None] * SLOTS + ranks
    sources = jnp.sum(jnp.where(mine, senders, 0), axis=0)
    projected, outgoing = project(
        z[None], slots, groups * SLOTS, shards, cosine, sine, w_query, w_key, w_value, bias
    )
    incoming = lax.all_to_all(outgoing, "group", split_axis=0, concat_axis=0, tiled=True)
    kv_pool = pick_pages(sources, incoming, page_count)

    info = jnp.stack([z.astype(jnp.int32), take_flag])
    pool = prefix_pool.reshape(2 * PREFIX, 2 * HD)

    work = (projected, bias, w_output)
    left, right, own_part, cache = attend(info, (4, 0), *work, pool, handed, split=True)
    ups, downs = {}, {}
    ups[3], downs[3] = attend(info, (3, 5), *work, cache)
    ups[2], downs[2], cache = attend(info, (2, 6), *work, pool, handed, after=(incoming,))
    ups[1], downs[1] = attend(info, (1, 7), *work, cache)
    going_up, going_down = shift(left, "tensor", 1), shift(right, "tensor", -1)
    for distance in (3, 2, 1):
        kernel = widen_kernel if distance == 3 else add_kernel
        going_up, going_down = combine(kernel, 2, "add_parts", ups[distance], downs[distance], going_up, going_down)
        going_up, going_down = shift(going_up, "tensor", 1), shift(going_down, "tensor", -1)
    (layer_out,) = combine(last_kernel, 1, "add_rows", rows, own_part, going_up, going_down)
    return (layer_out, kv_pool)


def solution(mesh):
    return jax.shard_map(
        local,
        mesh=mesh,
        in_specs=(
            P("group", None, "tensor", None),
            P(),
            P(None, "tensor"),
            P(None, "tensor"),
            P(None, "tensor"),
            P("tensor", None),
            P("group", None, "tensor"),
            P("group", None, None),
            P(),
            P(),
            P(),
        ),
        out_specs=(P(("group", "tensor"), None), P("group", None, "tensor")),
        check_vma=False,
    )
```

```python
import functools
import math

import jax
import jax.numpy as jnp
from jax import lax
from jax.experimental import pallas as pl
from jax.experimental.pallas import tpu as pltpu
from jax.sharding import PartitionSpec as P

HD = 128
PAGE = 8
BLOCK = 256
PREFIX = 8192
EPS = 1e-05
THETA = 500000.0

NT = 8
HEADS = 4
SHARD = BLOCK // NT
TILE = 256
KBLK = 512
NKB = PREFIX // KBLK
KEYS = PREFIX + BLOCK
NCH = 4
CHROWS = PREFIX // NCH
COPIES = 8
SLOTS = 2
NEW_KEYS = slice(HEADS * BLOCK, (HEADS + 1) * BLOCK)
NEW_VALUES = slice((HEADS + 1) * BLOCK, (HEADS + 2) * BLOCK)
MASKED = -1e30
EXP_SCALE = math.log2(math.e) / math.sqrt(HD)
MIB = 1 << 20
F32 = jnp.float32
BF16 = jnp.bfloat16

VMEM = pl.BlockSpec(memory_space=pltpu.VMEM)
SMEM = pl.BlockSpec(memory_space=pltpu.SMEM)
ANY = pl.BlockSpec(memory_space=pl.ANY)
HBM = pl.BlockSpec(memory_space=pltpu.HBM)


def shift(value, axis, distance):
    count = lax.axis_size(axis)
    return lax.ppermute(value, axis, [(i, (i + distance) % count) for i in range(count)])


def norm_kernel(take_ref, own_ref, handed_ref, gain_ref, slot_ref, *refs):
    rows_ref, normed_ref, _ = refs[-3:]
    take = take_ref[0] != 0
    rows = jnp.where(take, handed_ref[...].astype(F32), own_ref[...].astype(F32))
    rows_ref[...] = rows.astype(BF16)
    mean_square = jnp.mean(rows * rows, axis=-1, keepdims=True)
    normed_ref[...] = (rows * lax.rsqrt(mean_square + EPS) * gain_ref[...].astype(F32)).astype(BF16)


def choose_and_norm(take, own, handed, gain, slot, *before):
    return pl.pallas_call(
        norm_kernel,
        out_shape=[jax.ShapeDtypeStruct(own.shape, BF16)] * 2 + [jax.ShapeDtypeStruct(slot.shape, BF16)],
        in_specs=[SMEM, VMEM, VMEM, VMEM, HBM] + [ANY] * len(before),
        out_specs=[VMEM, VMEM, HBM],
        input_output_aliases={4: 2},
        compiler_params=pltpu.CompilerParams(vmem_limit_bytes=8 * MIB),
        cost_estimate=pl.CostEstimate(flops=10**6, bytes_accessed=10**6, transcendentals=0),
        name="choose_and_norm",
    )(take, own, handed, gain, slot, *before)


def later_kernel(count, *refs):
    for source_ref, out_ref in zip(refs[:count], refs[-count:]):
        out_ref[...] = source_ref[...]


def later(arrays, *before):
    return pl.pallas_call(
        functools.partial(later_kernel, len(arrays)),
        out_shape=[jax.ShapeDtypeStruct(x.shape, x.dtype) for x in arrays],
        in_specs=[VMEM] * len(arrays) + [ANY] * len(before),
        out_specs=[VMEM] * len(arrays),
        compiler_params=pltpu.CompilerParams(vmem_limit_bytes=4 * MIB),
        cost_estimate=pl.CostEstimate(flops=0, bytes_accessed=10**4, transcendentals=0),
        name="later",
    )(*arrays, *before)


def part_kernel(start, pool_hbm, *refs):
    out_hbm, stage_ref, in_sems, out_sems = refs[-4:]
    size = out_hbm.shape[0] // COPIES
    loads, stores = [], []
    for n in range(COPIES):
        part = pl.ds(n * size, size)
        source = pool_hbm.at[pl.ds(start + n * size, size)]
        loads.append(pltpu.make_async_copy(source, stage_ref.at[part], in_sems.at[n]))
        stores.append(pltpu.make_async_copy(stage_ref.at[part], out_hbm.at[part], out_sems.at[n]))
    for load in loads:
        load.start()
    for load, store in zip(loads, stores):
        load.wait()
        store.start()
    for store in stores:
        store.wait()


def second_slot(pool, *after):
    start = pool.shape[0] // 2
    shape = (start,) + pool.shape[1:]
    return pl.pallas_call(
        functools.partial(part_kernel, start),
        out_shape=jax.ShapeDtypeStruct(shape, BF16),
        in_specs=[HBM] + [ANY] * len(after),
        out_specs=HBM,
        scratch_shapes=[
            pltpu.VMEM(shape, BF16),
            pltpu.SemaphoreType.DMA((COPIES,)),
            pltpu.SemaphoreType.DMA((COPIES,)),
        ],
        compiler_params=pltpu.CompilerParams(vmem_limit_bytes=58 * MIB),
        cost_estimate=pl.CostEstimate(flops=0, bytes_accessed=9 * 10**6, transcendentals=0),
        name="second_slot",
    )(pool, *after)


def qkv_kernel(z_ref, slot_ref, *refs):
    shards = refs[:NT]
    cos_ref, sin_ref, wq_hbm, wk_hbm, wv_hbm, _, q_ref, send_ref = refs[NT : NT + 8]
    x_ref, wq_ref, wk_ref, wv_ref, shard_sem, sems = refs[NT + 8 :]
    z = z_ref[0]
    gathers = []
    for relative, shard in enumerate(shards):
        place = lax.rem(z + relative, NT)
        to = x_ref.at[pl.ds(pl.multiple_of(place * SHARD, SHARD), SHARD)]
        gathers.append(pltpu.make_async_copy(shard, to, shard_sem.at[relative]))
    copies = [
        pltpu.make_async_copy(src, dst, sems.at[n])
        for n, (src, dst) in enumerate([(wk_hbm, wk_ref), (wv_hbm, wv_ref)])
    ]
    half = wq_hbm.shape[0] // 2
    copies += [
        pltpu.make_async_copy(wq_hbm.at[pl.ds(n * half, half)], wq_ref.at[pl.ds(n * half, half)], sems.at[2 + n])
        for n in range(2)
    ]
    for copy in gathers + copies:
        copy.start()
    cosine = cos_ref[...]
    sine = sin_ref[...]

    def rotated(values):
        return values * cosine + pltpu.roll(values, HD // 2, 1) * sine

    for copy in gathers:
        copy.wait()
    copies[0].wait()
    new_keys = rotated(jnp.dot(x_ref[...], wk_ref[...], preferred_element_type=F32))
    q_ref[NEW_KEYS] = new_keys.astype(BF16)
    copies[1].wait()
    new_values = jnp.dot(x_ref[...], wv_ref[...], preferred_element_type=F32)
    q_ref[NEW_VALUES] = new_values.astype(BF16)
    for k in range(BLOCK // PAGE):
        slot = slot_ref[k]
        send_ref[slot, :, :HD] = new_keys[k * PAGE : (k + 1) * PAGE].astype(BF16)
        send_ref[slot, :, HD:] = new_values[k * PAGE : (k + 1) * PAGE].astype(BF16)
    copies[2].wait()
    copies[3].wait()
    for pair in range(HEADS // 2):
        both = jnp.dot(x_ref[...], wq_ref[:, pair * 2 * HD : (pair + 1) * 2 * HD], preferred_element_type=F32)
        for one in range(2):
            head = rotated(both[:, one * HD : (one + 1) * HD]).astype(BF16)
            n = pair * 2 + one
            for shard in range(NT):
                at = (shard * HEADS + n) * SHARD
                q_ref[at : at + SHARD] = head[shard * SHARD : (shard + 1) * SHARD]


def project(z, slots, count, shards, cosine, sine, w_query, w_key, w_value, bias):
    depth, query_width = w_query.shape
    return pl.pallas_call(
        qkv_kernel,
        out_shape=[
            jax.ShapeDtypeStruct(((HEADS + 2) * BLOCK, HD), BF16),
            jax.ShapeDtypeStruct((count, PAGE, 2 * HD), BF16),
        ],
        in_specs=[SMEM, SMEM] + [HBM] * NT + [VMEM] * 2 + [HBM] * 3 + [ANY],
        out_specs=[VMEM, VMEM],
        scratch_shapes=[
            pltpu.VMEM((BLOCK, depth), BF16),
            pltpu.VMEM(w_query.shape, BF16),
            pltpu.VMEM(w_key.shape, BF16),
            pltpu.VMEM(w_value.shape, BF16),
            pltpu.SemaphoreType.DMA((NT,)),
            pltpu.SemaphoreType.DMA((4,)),
        ],
        compiler_params=pltpu.CompilerParams(vmem_limit_bytes=58 * MIB),
        cost_estimate=pl.CostEstimate(
            flops=2 * BLOCK * depth * (query_width + 2 * HD), bytes_accessed=9 * 10**6, transcendentals=0
        ),
        name="project",
    )(z, slots, *shards, cosine, sine, w_query, w_key, w_value, bias)


def attention_kernel(picks, load, split, passed, info_ref, q_ref, bias_ref, *refs):
    if load:
        wo_hbm, pool_hbm, handed_hbm, *refs = refs
        kv_ref, att_ref, wo_ref, wo_sem, kv_sem = refs[-5:]
        out_refs = refs[passed : -5]
    else:
        wo_hbm, kv_ref, *refs = refs
        *out_refs, att_ref, wo_ref, wo_sem = refs[passed:]
    z = info_ref[0]
    take = info_ref[1]

    def cache_copy(n, source):
        part = pl.ds(n * CHROWS, CHROWS)
        return pltpu.make_async_copy(source.at[part], kv_ref.at[part], kv_sem.at[n])

    if load:

        @pl.when(take != 0)
        def _():
            for n in range(NCH):
                cache_copy(n, handed_hbm).start()

        @pl.when(take == 0)
        def _():
            for n in range(NCH):
                cache_copy(n, pool_hbm).start()

    wo_copy = pltpu.make_async_copy(wo_hbm, wo_ref, wo_sem)
    wo_copy.start()
    places = [lax.rem(z + pick, NT) for pick in picks]
    rows = HEADS * SHARD
    queries = jnp.concatenate([q_ref[pl.ds(pl.multiple_of(place * rows, rows), rows)] for place in places], axis=0)

    def scores(keys):
        return lax.dot_general(queries, keys, (((1,), (1,)), ((), ())), preferred_element_type=F32)

    def new_scores():
        block = scores(q_ref[NEW_KEYS])
        place = lax.broadcasted_iota(jnp.int32, (TILE, BLOCK), 0)
        row = place % SHARD + SHARD * jnp.where(place < TILE // 2, places[0], places[1])
        column = lax.broadcasted_iota(jnp.int32, (TILE, BLOCK), 1)
        return jnp.where(column <= row, block, MASKED)

    def stored_scores(n):
        if load and n % (CHROWS // KBLK) == 0:
            cache_copy(n // (CHROWS // KBLK), pool_hbm).wait()
        at = n * KBLK
        return scores(kv_ref[at : at + KBLK, :HD]) + bias_ref[:, at : at + KBLK]

    row_max = jnp.full((TILE, 1), MASKED, F32)
    total = jnp.zeros((TILE, HD), F32)
    sums = jnp.zeros((TILE, HD), F32)
    block = new_scores()
    values = q_ref[NEW_VALUES]
    for n in range(NKB + 1):
        following = stored_scores(n) if n < NKB else None
        lanes = [slice(c * HD, (c + 1) * HD) for c in range(block.shape[1] // HD)]
        top = block[:, lanes[0]]
        for lane in lanes[1:]:
            top = jnp.maximum(top, block[:, lane])
        raised = jnp.maximum(row_max, jnp.max(top, axis=1, keepdims=True))
        keep = jnp.exp2((row_max - raised) * EXP_SCALE)
        e = jnp.exp2((block - raised) * EXP_SCALE)
        total = total * keep
        for lane in lanes:
            total = total + e[:, lane]
        sums = sums * keep + jnp.dot(e.astype(BF16), values, preferred_element_type=F32)
        row_max = raised
        block = following
        values = kv_ref[n * KBLK : (n + 1) * KBLK, HD:] if n < NKB else None
    attended = (sums / jnp.sum(total, axis=1, keepdims=True)).astype(BF16)
    for half in range(2):
        for n in range(HEADS):
            at = half * HEADS * SHARD + n * SHARD
            to = half * SHARD
            att_ref[to : to + SHARD, n * HD : (n + 1) * HD] = attended[at : at + SHARD, :]
    wo_copy.wait()
    product = jnp.dot(att_ref[...], wo_ref[...], preferred_element_type=F32).astype(BF16)
    if split:
        columns = product.shape[1] // 2
        out_refs[0][...] = product[:SHARD, :columns]
        out_refs[1][...] = product[:SHARD, columns:]
        out_refs[2][...] = product[SHARD:]
    else:
        out_refs[0][...] = product[:SHARD]
        out_refs[1][...] = product[SHARD:]


def attend(info, picks, projected, bias, w_output, *held, split=False, keep=False, after=()):
    load = len(held) == 2
    width = w_output.shape[1]
    part = lambda columns: jax.ShapeDtypeStruct((SHARD, columns), BF16)
    out_shape = [part(width // 2), part(width // 2), part(width)] if split else [part(width)] * 2
    cache = (PREFIX, 2 * HD)
    scratch = [pltpu.VMEM(cache, BF16)] if load and not keep else []
    scratch += [pltpu.VMEM((2 * SHARD, HEADS * HD), BF16), pltpu.VMEM(w_output.shape, BF16), pltpu.SemaphoreType.DMA]
    if load:
        scratch += [pltpu.SemaphoreType.DMA((NCH,))]
    extra = [jax.ShapeDtypeStruct(cache, BF16)] if keep else []
    return pl.pallas_call(
        functools.partial(attention_kernel, picks, load, split, len(after)),
        out_shape=out_shape + extra,
        in_specs=[SMEM, VMEM, VMEM, HBM] + ([HBM, HBM] if load else [VMEM]) + [ANY] * len(after),
        out_specs=[VMEM] * len(out_shape + extra),
        scratch_shapes=scratch,
        compiler_params=pltpu.CompilerParams(vmem_limit_bytes=(46 if keep else 58 if load else 24) * MIB),
        cost_estimate=pl.CostEstimate(
            flops=8 * TILE * KEYS * HD, bytes_accessed=9 * 10**6, transcendentals=TILE * KEYS
        ),
        name="attend",
    )(info, projected, bias, w_output, *held, *after)


def plus(a, b):
    return a.astype(F32) + b.astype(F32)


def widen_kernel(up_ref, down_ref, from_left_ref, from_right_ref, *refs):
    up_out, down_out = refs[-2:]
    half = from_left_ref.shape[1]
    up_out[:, :half] = plus(up_ref[:, :half], from_left_ref[...]).astype(BF16)
    up_out[:, half:] = up_ref[:, half:]
    down_out[:, :half] = down_ref[:, :half]
    down_out[:, half:] = plus(down_ref[:, half:], from_right_ref[...]).astype(BF16)


def add_kernel(up_ref, down_ref, from_left_ref, from_right_ref, *refs):
    up_out, down_out = refs[-2:]
    up_out[...] = plus(up_ref[...], from_left_ref[...]).astype(BF16)
    down_out[...] = plus(down_ref[...], from_right_ref[...]).astype(BF16)


def last_kernel(rows_ref, part_ref, from_left_ref, from_right_ref, out_ref):
    branch = part_ref[...].astype(F32) + plus(from_left_ref[...], from_right_ref[...])
    out_ref[...] = (rows_ref[...].astype(F32) + branch).astype(BF16)


def combine(kernel, outputs, name, *arrays, after=()):
    shape = jax.ShapeDtypeStruct(arrays[0].shape, BF16)
    return pl.pallas_call(
        kernel,
        out_shape=[shape] * outputs,
        in_specs=[VMEM] * len(arrays) + [ANY] * len(after),
        out_specs=[VMEM] * outputs,
        compiler_params=pltpu.CompilerParams(vmem_limit_bytes=8 * MIB),
        cost_estimate=pl.CostEstimate(flops=10**6, bytes_accessed=2 * 10**6, transcendentals=0),
        name=name,
    )(*arrays, *after)


def pick_kernel(source_ref, pages_ref, out_ref):
    for k in range(out_ref.shape[0]):
        out_ref[k] = pages_ref[source_ref[k]]


def pick_pages(sources, pages, count):
    return pl.pallas_call(
        pick_kernel,
        out_shape=jax.ShapeDtypeStruct((count,) + pages.shape[1:], BF16),
        in_specs=[SMEM, VMEM],
        out_specs=VMEM,
        compiler_params=pltpu.CompilerParams(vmem_limit_bytes=4 * MIB),
        cost_estimate=pl.CostEstimate(flops=0, bytes_accessed=4 * 10**5, transcendentals=0),
        name="pick_pages",
    )(sources, pages)


def local(
    hidden,
    norm_gain,
    w_query,
    w_key,
    w_value,
    w_output,
    prefix_pool,
    page_table,
    prefix_len,
    source,
    decode_owner,
):
    groups = lax.axis_size("group")
    group = lax.axis_index("group")
    z = lax.axis_index("tensor")
    lower = (group + groups - 1) % groups
    take = source[group] == lower
    take_flag = take.astype(jnp.int32)

    sent_rows = hidden[0, 1]
    sent_table = page_table[0, 1]
    handed_rows = shift(sent_rows, "group", 1)
    handed_table = shift(sent_table, "group", 1)
    pages = prefix_pool.shape[0] // 2
    slot = second_slot(prefix_pool, sent_rows, sent_table)
    rows, normed, slot = choose_and_norm(
        take_flag[None], hidden[0, 0], handed_rows, norm_gain[None], slot, handed_table[None]
    )
    handed = shift(slot, "group", 1).reshape(PREFIX, 2 * HD)

    up, down = [normed], [normed]
    for _ in range(NT // 2 - 1):
        up.append(shift(up[-1], "tensor", 1))
        down.append(shift(down[-1], "tensor", -1))
    prefix_len, decode_owner, handed_table = later((prefix_len, decode_owner, handed_table[None]), up[1])
    count = jnp.where(take, prefix_len[lower, 1], prefix_len[group, 0])
    half = SHARD // 2
    opposite = jnp.concatenate([shift(up[-1][:half], "tensor", 1), shift(down[-1][half:], "tensor", -1)], axis=0)
    shards = down + [opposite] + up[:0:-1]

    table = jnp.where(take, handed_table[0], page_table[0, 0])
    order = jnp.arange(pages, dtype=jnp.int32)
    place = jnp.sum(jnp.where(table[:, None] == order[None, :], order[:, None], 0), axis=0)
    position = place[:, None] * PAGE + jnp.arange(PAGE, dtype=jnp.int32)[None, :]
    bias = jnp.where(position < count, 0.0, MASKED).astype(F32).reshape(1, PREFIX)

    positions = (count + jnp.arange(BLOCK, dtype=jnp.int32)).astype(F32)
    frequency = THETA ** (-(jnp.arange(HD // 2, dtype=F32) * 2.0) / HD)
    angles = positions[:, None] * frequency
    cosine = jnp.cos(angles)
    sine = jnp.sin(angles)
    cosine = jnp.concatenate([cosine, cosine], axis=1)
    sine = jnp.concatenate([-sine, sine], axis=1)

    page_count = BLOCK // PAGE
    ids = jnp.arange(page_count, dtype=jnp.int32)
    same = jnp.logical_and(decode_owner[:, :, None] == decode_owner[:, None, :], ids[None, None, :] < ids[None, :, None])
    ranks = jnp.sum(same.astype(jnp.int32), axis=-1)
    slots = decode_owner[group] * SLOTS + ranks[group]
    mine = decode_owner == group
    senders = jnp.arange(groups, dtype=jnp.int32)[:, None] * SLOTS + ranks
    sources = jnp.sum(jnp.where(mine, senders, 0), axis=0)
    projected, outgoing = project(
        z[None], slots, groups * SLOTS, shards, cosine, sine, w_query, w_key, w_value, bias
    )
    incoming = lax.all_to_all(outgoing, "group", split_axis=0, concat_axis=0, tiled=True)
    kv_pool = pick_pages(sources, incoming, page_count)

    info = jnp.stack([z.astype(jnp.int32), take_flag])
    pool = prefix_pool.reshape(2 * PREFIX, 2 * HD)

    work = (projected, bias, w_output)
    left, right, own_part, cache = attend(info, (4, 0), *work, pool, handed, split=True, keep=True)
    ups, downs = {}, {}
    for distance in (3, 2, 1):
        held = (cache,) if distance > 1 else (pool, handed)
        ups[distance], downs[distance] = attend(info, (distance, NT - distance), *work, *held)
    going_up, going_down = shift(left, "tensor", 1), shift(right, "tensor", -1)
    for distance in (3, 2, 1):
        kernel = widen_kernel if distance == 3 else add_kernel
        after = (incoming,) if distance == 1 else ()
        going_up, going_down = combine(
            kernel, 2, "add_parts", ups[distance], downs[distance], going_up, going_down, after=after
        )
        going_up, going_down = shift(going_up, "tensor", 1), shift(going_down, "tensor", -1)
    (layer_out,) = combine(last_kernel, 1, "add_rows", rows, own_part, going_up, going_down)
    return (layer_out, kv_pool)


def solution(mesh):
    return jax.shard_map(
        local,
        mesh=mesh,
        in_specs=(
            P("group", None, "tensor", None),
            P(),
            P(None, "tensor"),
            P(None, "tensor"),
            P(None, "tensor"),
            P("tensor", None),
            P("group", None, "tensor"),
            P("group", None, None),
            P(),
            P(),
            P(),
        ),
        out_specs=(P(("group", "tensor"), None), P("group", None, "tensor")),
        check_vma=False,
    )
```

```python
import functools
import math

import jax
import jax.numpy as jnp
from jax import lax
from jax.experimental import pallas as pl
from jax.experimental.pallas import tpu as pltpu
from jax.sharding import PartitionSpec as P

HD = 128
PAGE = 8
BLOCK = 256
PREFIX = 8192
EPS = 1e-05
THETA = 500000.0

NT = 8
HEADS = 4
SHARD = BLOCK // NT
TILE = 256
KBLK = 512
KEYS = PREFIX + BLOCK
NCH = 4
CHROWS = PREFIX // NCH
COPIES = 8
SLOTS = 2
NEW_KEYS = slice(HEADS * BLOCK, (HEADS + 1) * BLOCK)
NEW_VALUES = slice((HEADS + 1) * BLOCK, (HEADS + 2) * BLOCK)
MASKED = -1e30
EXP_SCALE = math.log2(math.e) / math.sqrt(HD)
MIB = 1 << 20
F32 = jnp.float32
BF16 = jnp.bfloat16

VMEM = pl.BlockSpec(memory_space=pltpu.VMEM)
SMEM = pl.BlockSpec(memory_space=pltpu.SMEM)
ANY = pl.BlockSpec(memory_space=pl.ANY)
HBM = pl.BlockSpec(memory_space=pltpu.HBM)


def shift(value, axis, distance):
    count = lax.axis_size(axis)
    return lax.ppermute(value, axis, [(i, (i + distance) % count) for i in range(count)])


def norm_kernel(take_ref, own_ref, handed_ref, gain_ref, slot_ref, *refs):
    rows_ref, normed_ref, _ = refs[-3:]
    take = take_ref[0] != 0
    rows = jnp.where(take, handed_ref[...].astype(F32), own_ref[...].astype(F32))
    rows_ref[...] = rows.astype(BF16)
    mean_square = jnp.mean(rows * rows, axis=-1, keepdims=True)
    normed_ref[...] = (rows * lax.rsqrt(mean_square + EPS) * gain_ref[...].astype(F32)).astype(BF16)


def choose_and_norm(take, own, handed, gain, slot, *before):
    return pl.pallas_call(
        norm_kernel,
        out_shape=[jax.ShapeDtypeStruct(own.shape, BF16)] * 2 + [jax.ShapeDtypeStruct(slot.shape, BF16)],
        in_specs=[SMEM, VMEM, VMEM, VMEM, HBM] + [ANY] * len(before),
        out_specs=[VMEM, VMEM, HBM],
        input_output_aliases={4: 2},
        compiler_params=pltpu.CompilerParams(vmem_limit_bytes=8 * MIB),
        cost_estimate=pl.CostEstimate(flops=10**6, bytes_accessed=10**6, transcendentals=0),
        name="choose_and_norm",
    )(take, own, handed, gain, slot, *before)


def later_kernel(count, *refs):
    for source_ref, out_ref in zip(refs[:count], refs[-count:]):
        out_ref[...] = source_ref[...]


def later(arrays, *before):
    return pl.pallas_call(
        functools.partial(later_kernel, len(arrays)),
        out_shape=[jax.ShapeDtypeStruct(x.shape, x.dtype) for x in arrays],
        in_specs=[VMEM] * len(arrays) + [ANY] * len(before),
        out_specs=[VMEM] * len(arrays),
        compiler_params=pltpu.CompilerParams(vmem_limit_bytes=4 * MIB),
        cost_estimate=pl.CostEstimate(flops=0, bytes_accessed=10**4, transcendentals=0),
        name="later",
    )(*arrays, *before)


def part_kernel(start, pool_hbm, *refs):
    out_hbm, stage_ref, in_sems, out_sems = refs[-4:]
    size = out_hbm.shape[0] // COPIES
    loads, stores = [], []
    for n in range(COPIES):
        part = pl.ds(n * size, size)
        source = pool_hbm.at[pl.ds(start + n * size, size)]
        loads.append(pltpu.make_async_copy(source, stage_ref.at[part], in_sems.at[n]))
        stores.append(pltpu.make_async_copy(stage_ref.at[part], out_hbm.at[part], out_sems.at[n]))
    for load in loads:
        load.start()
    for load, store in zip(loads, stores):
        load.wait()
        store.start()
    for store in stores:
        store.wait()


def second_slot(pool, *after):
    start = pool.shape[0] // 2
    shape = (start,) + pool.shape[1:]
    return pl.pallas_call(
        functools.partial(part_kernel, start),
        out_shape=jax.ShapeDtypeStruct(shape, BF16),
        in_specs=[HBM] + [ANY] * len(after),
        out_specs=HBM,
        scratch_shapes=[
            pltpu.VMEM(shape, BF16),
            pltpu.SemaphoreType.DMA((COPIES,)),
            pltpu.SemaphoreType.DMA((COPIES,)),
        ],
        compiler_params=pltpu.CompilerParams(vmem_limit_bytes=58 * MIB),
        cost_estimate=pl.CostEstimate(flops=0, bytes_accessed=9 * 10**6, transcendentals=0),
        name="second_slot",
    )(pool, *after)


def qkv_kernel(z_ref, slot_ref, *refs):
    shards = refs[:NT]
    cos_ref, sin_ref, wq_hbm, wk_hbm, wv_hbm, _, q_ref, send_ref = refs[NT : NT + 8]
    x_ref, wq_ref, wk_ref, wv_ref, shard_sem, sems = refs[NT + 8 :]
    z = z_ref[0]
    gathers = []
    for relative, shard in enumerate(shards):
        place = lax.rem(z + relative, NT)
        to = x_ref.at[pl.ds(pl.multiple_of(place * SHARD, SHARD), SHARD)]
        gathers.append(pltpu.make_async_copy(shard, to, shard_sem.at[relative]))
    copies = [
        pltpu.make_async_copy(src, dst, sems.at[n])
        for n, (src, dst) in enumerate([(wk_hbm, wk_ref), (wv_hbm, wv_ref)])
    ]
    half = wq_hbm.shape[0] // 2
    copies += [
        pltpu.make_async_copy(wq_hbm.at[pl.ds(n * half, half)], wq_ref.at[pl.ds(n * half, half)], sems.at[2 + n])
        for n in range(2)
    ]
    for copy in gathers + copies:
        copy.start()
    cosine = cos_ref[...]
    sine = sin_ref[...]

    def rotated(values):
        return values * cosine + pltpu.roll(values, HD // 2, 1) * sine

    for copy in gathers:
        copy.wait()
    copies[0].wait()
    new_keys = rotated(jnp.dot(x_ref[...], wk_ref[...], preferred_element_type=F32))
    q_ref[NEW_KEYS] = new_keys.astype(BF16)
    copies[1].wait()
    new_values = jnp.dot(x_ref[...], wv_ref[...], preferred_element_type=F32)
    q_ref[NEW_VALUES] = new_values.astype(BF16)
    for k in range(BLOCK // PAGE):
        slot = slot_ref[k]
        send_ref[slot, :, :HD] = new_keys[k * PAGE : (k + 1) * PAGE].astype(BF16)
        send_ref[slot, :, HD:] = new_values[k * PAGE : (k + 1) * PAGE].astype(BF16)
    copies[2].wait()
    copies[3].wait()
    for pair in range(HEADS // 2):
        both = jnp.dot(x_ref[...], wq_ref[:, pair * 2 * HD : (pair + 1) * 2 * HD], preferred_element_type=F32)
        for one in range(2):
            head = rotated(both[:, one * HD : (one + 1) * HD]).astype(BF16)
            n = pair * 2 + one
            for shard in range(NT):
                at = (shard * HEADS + n) * SHARD
                q_ref[at : at + SHARD] = head[shard * SHARD : (shard + 1) * SHARD]


def project(z, slots, count, shards, cosine, sine, w_query, w_key, w_value, bias):
    depth, query_width = w_query.shape
    return pl.pallas_call(
        qkv_kernel,
        out_shape=[
            jax.ShapeDtypeStruct(((HEADS + 2) * BLOCK, HD), BF16),
            jax.ShapeDtypeStruct((count, PAGE, 2 * HD), BF16),
        ],
        in_specs=[SMEM, SMEM] + [HBM] * NT + [VMEM] * 2 + [HBM] * 3 + [ANY],
        out_specs=[VMEM, VMEM],
        scratch_shapes=[
            pltpu.VMEM((BLOCK, depth), BF16),
            pltpu.VMEM(w_query.shape, BF16),
            pltpu.VMEM(w_key.shape, BF16),
            pltpu.VMEM(w_value.shape, BF16),
            pltpu.SemaphoreType.DMA((NT,)),
            pltpu.SemaphoreType.DMA((4,)),
        ],
        compiler_params=pltpu.CompilerParams(vmem_limit_bytes=58 * MIB),
        cost_estimate=pl.CostEstimate(
            flops=2 * BLOCK * depth * (query_width + 2 * HD), bytes_accessed=9 * 10**6, transcendentals=0
        ),
        name="project",
    )(z, slots, *shards, cosine, sine, w_query, w_key, w_value, bias)


def attention_kernel(picks, load, split, passed, info_ref, q_ref, bias_ref, *refs):
    if load:
        wo_hbm, pool_hbm, handed_hbm, *refs = refs
        kv_ref, att_ref, wo_ref, wo_sem, kv_sem = refs[-5:]
        out_refs = refs[passed : -5]
    else:
        wo_hbm, kv_ref, *refs = refs
        *out_refs, att_ref, wo_ref, wo_sem = refs[passed:]
    z = info_ref[0]
    take = info_ref[1]

    def cache_copy(n, source):
        part = pl.ds(pl.multiple_of(n * CHROWS, CHROWS), CHROWS)
        return pltpu.make_async_copy(source.at[part], kv_ref.at[part], kv_sem.at[n])

    if load:

        @pl.when(take != 0)
        def _():
            for n in range(NCH):
                cache_copy(n, handed_hbm).start()

        @pl.when(take == 0)
        def _():
            for n in range(NCH):
                cache_copy(n, pool_hbm).start()

    wo_copy = pltpu.make_async_copy(wo_hbm, wo_ref, wo_sem)
    wo_copy.start()
    places = [lax.rem(z + pick, NT) for pick in picks]
    rows = HEADS * SHARD
    queries = jnp.concatenate([q_ref[pl.ds(pl.multiple_of(place * rows, rows), rows)] for place in places], axis=0)

    def scores(keys):
        return lax.dot_general(queries, keys, (((1,), (1,)), ((), ())), preferred_element_type=F32)

    def new_scores():
        block = scores(q_ref[NEW_KEYS])
        place = lax.broadcasted_iota(jnp.int32, (TILE, BLOCK), 0)
        row = place % SHARD + SHARD * jnp.where(place < TILE // 2, places[0], places[1])
        column = lax.broadcasted_iota(jnp.int32, (TILE, BLOCK), 1)
        return jnp.where(column <= row, block, MASKED)

    def stored_scores(at):
        at = pl.multiple_of(at, KBLK)
        return scores(kv_ref[pl.ds(at, KBLK), :HD]) + bias_ref[:, pl.ds(at, KBLK)]

    def fold(block, values, row_max, total, sums):
        lanes = [slice(c * HD, (c + 1) * HD) for c in range(block.shape[1] // HD)]
        top = block[:, lanes[0]]
        for lane in lanes[1:]:
            top = jnp.maximum(top, block[:, lane])
        raised = jnp.maximum(row_max, jnp.max(top, axis=1, keepdims=True))
        keep = jnp.exp2((row_max - raised) * EXP_SCALE)
        e = jnp.exp2((block - raised) * EXP_SCALE)
        total = total * keep
        for lane in lanes:
            total = total + e[:, lane]
        return raised, total, sums * keep + jnp.dot(e.astype(BF16), values, preferred_element_type=F32)

    def chunk(c, carry):
        base = pl.multiple_of(c * CHROWS, CHROWS)
        if load:
            cache_copy(c, pool_hbm).wait()
        block = stored_scores(base)
        for n in range(CHROWS // KBLK):
            following = stored_scores(base + (n + 1) * KBLK) if (n + 1) * KBLK < CHROWS else None
            values = kv_ref[pl.ds(pl.multiple_of(base + n * KBLK, KBLK), KBLK), HD:]
            carry = fold(block, values, *carry)
            block = following
        return carry

    zeros = jnp.zeros((TILE, HD), F32)
    carry = fold(new_scores(), q_ref[NEW_VALUES], jnp.full((TILE, 1), MASKED, F32), zeros, zeros)
    _, total, sums = lax.fori_loop(0, NCH, chunk, carry)
    attended = (sums / jnp.sum(total, axis=1, keepdims=True)).astype(BF16)
    for half in range(2):
        for n in range(HEADS):
            at = half * HEADS * SHARD + n * SHARD
            to = half * SHARD
            att_ref[to : to + SHARD, n * HD : (n + 1) * HD] = attended[at : at + SHARD, :]
    wo_copy.wait()
    product = jnp.dot(att_ref[...], wo_ref[...], preferred_element_type=F32).astype(BF16)
    if split:
        columns = product.shape[1] // 2
        out_refs[0][...] = product[:SHARD, :columns]
        out_refs[1][...] = product[:SHARD, columns:]
        out_refs[2][...] = product[SHARD:]
    else:
        out_refs[0][...] = product[:SHARD]
        out_refs[1][...] = product[SHARD:]


def attend(info, picks, projected, bias, w_output, *held, split=False, after=()):
    load = len(held) == 2
    width = w_output.shape[1]
    part = lambda columns: jax.ShapeDtypeStruct((SHARD, columns), BF16)
    out_shape = [part(width // 2), part(width // 2), part(width)] if split else [part(width)] * 2
    scratch = [pltpu.VMEM((2 * SHARD, HEADS * HD), BF16), pltpu.VMEM(w_output.shape, BF16), pltpu.SemaphoreType.DMA]
    if load:
        scratch += [pltpu.SemaphoreType.DMA((NCH,))]
    extra = [jax.ShapeDtypeStruct((PREFIX, 2 * HD), BF16)] if load else []
    return pl.pallas_call(
        functools.partial(attention_kernel, picks, load, split, len(after)),
        out_shape=out_shape + extra,
        in_specs=[SMEM, VMEM, VMEM, HBM] + ([HBM, HBM] if load else [VMEM]) + [ANY] * len(after),
        out_specs=[VMEM] * len(out_shape + extra),
        scratch_shapes=scratch,
        compiler_params=pltpu.CompilerParams(vmem_limit_bytes=(46 if load else 24) * MIB),
        cost_estimate=pl.CostEstimate(
            flops=8 * TILE * KEYS * HD, bytes_accessed=9 * 10**6, transcendentals=TILE * KEYS
        ),
        name="attend",
    )(info, projected, bias, w_output, *held, *after)


def plus(a, b):
    return a.astype(F32) + b.astype(F32)


def widen_kernel(up_ref, down_ref, from_left_ref, from_right_ref, up_out, down_out):
    half = from_left_ref.shape[1]
    up_out[:, :half] = plus(up_ref[:, :half], from_left_ref[...]).astype(BF16)
    up_out[:, half:] = up_ref[:, half:]
    down_out[:, :half] = down_ref[:, :half]
    down_out[:, half:] = plus(down_ref[:, half:], from_right_ref[...]).astype(BF16)


def add_kernel(up_ref, down_ref, from_left_ref, from_right_ref, up_out, down_out):
    up_out[...] = plus(up_ref[...], from_left_ref[...]).astype(BF16)
    down_out[...] = plus(down_ref[...], from_right_ref[...]).astype(BF16)


def last_kernel(rows_ref, part_ref, from_left_ref, from_right_ref, out_ref):
    branch = part_ref[...].astype(F32) + plus(from_left_ref[...], from_right_ref[...])
    out_ref[...] = (rows_ref[...].astype(F32) + branch).astype(BF16)


def combine(kernel, outputs, name, *arrays):
    shape = jax.ShapeDtypeStruct(arrays[0].shape, BF16)
    return pl.pallas_call(
        kernel,
        out_shape=[shape] * outputs,
        in_specs=[VMEM] * len(arrays),
        out_specs=[VMEM] * outputs,
        compiler_params=pltpu.CompilerParams(vmem_limit_bytes=8 * MIB),
        cost_estimate=pl.CostEstimate(flops=10**6, bytes_accessed=2 * 10**6, transcendentals=0),
        name=name,
    )(*arrays)


def pick_kernel(source_ref, pages_ref, out_ref):
    for k in range(out_ref.shape[0]):
        out_ref[k] = pages_ref[source_ref[k]]


def pick_pages(sources, pages, count):
    return pl.pallas_call(
        pick_kernel,
        out_shape=jax.ShapeDtypeStruct((count,) + pages.shape[1:], BF16),
        in_specs=[SMEM, VMEM],
        out_specs=VMEM,
        compiler_params=pltpu.CompilerParams(vmem_limit_bytes=4 * MIB),
        cost_estimate=pl.CostEstimate(flops=0, bytes_accessed=4 * 10**5, transcendentals=0),
        name="pick_pages",
    )(sources, pages)


def local(
    hidden,
    norm_gain,
    w_query,
    w_key,
    w_value,
    w_output,
    prefix_pool,
    page_table,
    prefix_len,
    source,
    decode_owner,
):
    groups = lax.axis_size("group")
    group = lax.axis_index("group")
    z = lax.axis_index("tensor")
    lower = (group + groups - 1) % groups
    take = source[group] == lower
    take_flag = take.astype(jnp.int32)

    sent_rows = hidden[0, 1]
    sent_table = page_table[0, 1]
    handed_rows = shift(sent_rows, "group", 1)
    handed_table = shift(sent_table, "group", 1)
    pages = prefix_pool.shape[0] // 2
    slot = second_slot(prefix_pool, sent_rows, sent_table)
    rows, normed, slot = choose_and_norm(
        take_flag[None], hidden[0, 0], handed_rows, norm_gain[None], slot, handed_table[None]
    )
    handed = shift(slot, "group", 1).reshape(PREFIX, 2 * HD)

    up, down = [normed], [normed]
    for _ in range(NT // 2 - 1):
        up.append(shift(up[-1], "tensor", 1))
        down.append(shift(down[-1], "tensor", -1))
    prefix_len, decode_owner, handed_table = later((prefix_len, decode_owner, handed_table[None]), up[1])
    count = jnp.where(take, prefix_len[lower, 1], prefix_len[group, 0])
    half = SHARD // 2
    opposite = jnp.concatenate([shift(up[-1][:half], "tensor", 1), shift(down[-1][half:], "tensor", -1)], axis=0)
    shards = down + [opposite] + up[:0:-1]

    table = jnp.where(take, handed_table[0], page_table[0, 0])
    order = jnp.arange(pages, dtype=jnp.int32)
    place = jnp.sum(jnp.where(table[:, None] == order[None, :], order[:, None], 0), axis=0)
    position = place[:, None] * PAGE + jnp.arange(PAGE, dtype=jnp.int32)[None, :]
    bias = jnp.where(position < count, 0.0, MASKED).astype(F32).reshape(1, PREFIX)

    positions = (count + jnp.arange(BLOCK, dtype=jnp.int32)).astype(F32)
    frequency = THETA ** (-(jnp.arange(HD // 2, dtype=F32) * 2.0) / HD)
    angles = positions[:, None] * frequency
    cosine = jnp.cos(angles)
    sine = jnp.sin(angles)
    cosine = jnp.concatenate([cosine, cosine], axis=1)
    sine = jnp.concatenate([-sine, sine], axis=1)

    page_count = BLOCK // PAGE
    ids = jnp.arange(page_count, dtype=jnp.int32)
    same = jnp.logical_and(decode_owner[:, :, None] == decode_owner[:, None, :], ids[None, None, :] < ids[None, :, None])
    ranks = jnp.sum(same.astype(jnp.int32), axis=-1)
    slots = decode_owner[group] * SLOTS + ranks[group]
    mine = decode_owner == group
    senders = jnp.arange(groups, dtype=jnp.int32)[:, None] * SLOTS + ranks
    sources = jnp.sum(jnp.where(mine, senders, 0), axis=0)
    projected, outgoing = project(
        z[None], slots, groups * SLOTS, shards, cosine, sine, w_query, w_key, w_value, bias
    )
    incoming = lax.all_to_all(outgoing, "group", split_axis=0, concat_axis=0, tiled=True)
    kv_pool = pick_pages(sources, incoming, page_count)

    info = jnp.stack([z.astype(jnp.int32), take_flag])
    pool = prefix_pool.reshape(2 * PREFIX, 2 * HD)

    work = (projected, bias, w_output)
    left, right, own_part, cache = attend(info, (4, 0), *work, pool, handed, split=True)
    ups, downs = {}, {}
    ups[3], downs[3] = attend(info, (3, 5), *work, cache)
    ups[2], downs[2], cache = attend(info, (2, 6), *work, pool, handed, after=(incoming,))
    ups[1], downs[1] = attend(info, (1, 7), *work, cache)
    going_up, going_down = shift(left, "tensor", 1), shift(right, "tensor", -1)
    for distance in (3, 2, 1):
        kernel = widen_kernel if distance == 3 else add_kernel
        going_up, going_down = combine(kernel, 2, "add_parts", ups[distance], downs[distance], going_up, going_down)
        going_up, going_down = shift(going_up, "tensor", 1), shift(going_down, "tensor", -1)
    (layer_out,) = combine(last_kernel, 1, "add_rows", rows, own_part, going_up, going_down)
    return (layer_out, kv_pool)


def solution(mesh):
    return jax.shard_map(
        local,
        mesh=mesh,
        in_specs=(
            P("group", None, "tensor", None),
            P(),
            P(None, "tensor"),
            P(None, "tensor"),
            P(None, "tensor"),
            P("tensor", None),
            P("group", None, "tensor"),
            P("group", None, None),
            P(),
            P(),
            P(),
        ),
        out_specs=(P(("group", "tensor"), None), P("group", None, "tensor")),
        check_vma=False,
    )
```

```python
import functools
import math

import jax
import jax.numpy as jnp
from jax import lax
from jax.experimental import pallas as pl
from jax.experimental.pallas import tpu as pltpu
from jax.sharding import PartitionSpec as P

HD = 128
PAGE = 8
BLOCK = 256
PREFIX = 8192
EPS = 1e-05
THETA = 500000.0

NT = 8
HEADS = 4
SHARD = BLOCK // NT
TILE = 256
KBLK = 512
KEYS = PREFIX + BLOCK
NCH = 4
CHROWS = PREFIX // NCH
COPIES = 8
SLOTS = 2
NEW_KEYS = slice(HEADS * BLOCK, (HEADS + 1) * BLOCK)
NEW_VALUES = slice((HEADS + 1) * BLOCK, (HEADS + 2) * BLOCK)
MASKED = -1e30
EXP_SCALE = math.log2(math.e) / math.sqrt(HD)
MIB = 1 << 20
F32 = jnp.float32
BF16 = jnp.bfloat16

VMEM = pl.BlockSpec(memory_space=pltpu.VMEM)
SMEM = pl.BlockSpec(memory_space=pltpu.SMEM)
ANY = pl.BlockSpec(memory_space=pl.ANY)
HBM = pl.BlockSpec(memory_space=pltpu.HBM)


def shift(value, axis, distance):
    count = lax.axis_size(axis)
    return lax.ppermute(value, axis, [(i, (i + distance) % count) for i in range(count)])


def norm_kernel(take_ref, own_ref, handed_ref, gain_ref, slot_ref, *refs):
    rows_ref, normed_ref, _ = refs[-3:]
    take = take_ref[0] != 0
    rows = jnp.where(take, handed_ref[...].astype(F32), own_ref[...].astype(F32))
    rows_ref[...] = rows.astype(BF16)
    mean_square = jnp.mean(rows * rows, axis=-1, keepdims=True)
    normed_ref[...] = (rows * lax.rsqrt(mean_square + EPS) * gain_ref[...].astype(F32)).astype(BF16)


def choose_and_norm(take, own, handed, gain, slot, *before):
    return pl.pallas_call(
        norm_kernel,
        out_shape=[jax.ShapeDtypeStruct(own.shape, BF16)] * 2 + [jax.ShapeDtypeStruct(slot.shape, BF16)],
        in_specs=[SMEM, VMEM, VMEM, VMEM, HBM] + [ANY] * len(before),
        out_specs=[VMEM, VMEM, HBM],
        input_output_aliases={4: 2},
        compiler_params=pltpu.CompilerParams(vmem_limit_bytes=8 * MIB),
        cost_estimate=pl.CostEstimate(flops=10**6, bytes_accessed=10**6, transcendentals=0),
        name="choose_and_norm",
    )(take, own, handed, gain, slot, *before)


def later_kernel(count, *refs):
    for source_ref, out_ref in zip(refs[:count], refs[-count:]):
        out_ref[...] = source_ref[...]


def later(arrays, *before):
    return pl.pallas_call(
        functools.partial(later_kernel, len(arrays)),
        out_shape=[jax.ShapeDtypeStruct(x.shape, x.dtype) for x in arrays],
        in_specs=[VMEM] * len(arrays) + [ANY] * len(before),
        out_specs=[VMEM] * len(arrays),
        compiler_params=pltpu.CompilerParams(vmem_limit_bytes=4 * MIB),
        cost_estimate=pl.CostEstimate(flops=0, bytes_accessed=10**4, transcendentals=0),
        name="later",
    )(*arrays, *before)


def part_kernel(start, pool_hbm, *refs):
    out_hbm, stage_ref, in_sems, out_sems = refs[-4:]
    size = out_hbm.shape[0] // COPIES
    loads, stores = [], []
    for n in range(COPIES):
        part = pl.ds(n * size, size)
        source = pool_hbm.at[pl.ds(start + n * size, size)]
        loads.append(pltpu.make_async_copy(source, stage_ref.at[part], in_sems.at[n]))
        stores.append(pltpu.make_async_copy(stage_ref.at[part], out_hbm.at[part], out_sems.at[n]))
    for load in loads:
        load.start()
    for load, store in zip(loads, stores):
        load.wait()
        store.start()
    for store in stores:
        store.wait()


def second_slot(pool, *after):
    start = pool.shape[0] // 2
    shape = (start,) + pool.shape[1:]
    return pl.pallas_call(
        functools.partial(part_kernel, start),
        out_shape=jax.ShapeDtypeStruct(shape, BF16),
        in_specs=[HBM] + [ANY] * len(after),
        out_specs=HBM,
        scratch_shapes=[
            pltpu.VMEM(shape, BF16),
            pltpu.SemaphoreType.DMA((COPIES,)),
            pltpu.SemaphoreType.DMA((COPIES,)),
        ],
        compiler_params=pltpu.CompilerParams(vmem_limit_bytes=58 * MIB),
        cost_estimate=pl.CostEstimate(flops=0, bytes_accessed=9 * 10**6, transcendentals=0),
        name="second_slot",
    )(pool, *after)


def qkv_kernel(z_ref, slot_ref, *refs):
    shards = refs[:NT]
    cos_ref, sin_ref, wq_hbm, wk_hbm, wv_hbm, _, q_ref, send_ref = refs[NT : NT + 8]
    x_ref, wq_ref, wk_ref, wv_ref, shard_sem, sems = refs[NT + 8 :]
    z = z_ref[0]
    gathers = []
    for relative, shard in enumerate(shards):
        place = lax.rem(z + relative, NT)
        to = x_ref.at[pl.ds(pl.multiple_of(place * SHARD, SHARD), SHARD)]
        gathers.append(pltpu.make_async_copy(shard, to, shard_sem.at[relative]))
    copies = [
        pltpu.make_async_copy(src, dst, sems.at[n])
        for n, (src, dst) in enumerate([(wk_hbm, wk_ref), (wv_hbm, wv_ref)])
    ]
    half = wq_hbm.shape[0] // 2
    copies += [
        pltpu.make_async_copy(wq_hbm.at[pl.ds(n * half, half)], wq_ref.at[pl.ds(n * half, half)], sems.at[2 + n])
        for n in range(2)
    ]
    for copy in gathers + copies:
        copy.start()
    cosine = cos_ref[...]
    sine = sin_ref[...]

    def rotated(values):
        return values * cosine + pltpu.roll(values, HD // 2, 1) * sine

    for copy in gathers:
        copy.wait()
    copies[0].wait()
    new_keys = rotated(jnp.dot(x_ref[...], wk_ref[...], preferred_element_type=F32))
    q_ref[NEW_KEYS] = new_keys.astype(BF16)
    copies[1].wait()
    new_values = jnp.dot(x_ref[...], wv_ref[...], preferred_element_type=F32)
    q_ref[NEW_VALUES] = new_values.astype(BF16)
    for k in range(BLOCK // PAGE):
        slot = slot_ref[k]
        send_ref[slot, :, :HD] = new_keys[k * PAGE : (k + 1) * PAGE].astype(BF16)
        send_ref[slot, :, HD:] = new_values[k * PAGE : (k + 1) * PAGE].astype(BF16)
    copies[2].wait()
    copies[3].wait()
    for pair in range(HEADS // 2):
        both = jnp.dot(x_ref[...], wq_ref[:, pair * 2 * HD : (pair + 1) * 2 * HD], preferred_element_type=F32)
        for one in range(2):
            head = rotated(both[:, one * HD : (one + 1) * HD]).astype(BF16)
            n = pair * 2 + one
            for shard in range(NT):
                at = (shard * HEADS + n) * SHARD
                q_ref[at : at + SHARD] = head[shard * SHARD : (shard + 1) * SHARD]


def project(z, slots, count, shards, cosine, sine, w_query, w_key, w_value, bias):
    depth, query_width = w_query.shape
    return pl.pallas_call(
        qkv_kernel,
        out_shape=[
            jax.ShapeDtypeStruct(((HEADS + 2) * BLOCK, HD), BF16),
            jax.ShapeDtypeStruct((count, PAGE, 2 * HD), BF16),
        ],
        in_specs=[SMEM, SMEM] + [HBM] * NT + [VMEM] * 2 + [HBM] * 3 + [ANY],
        out_specs=[VMEM, VMEM],
        scratch_shapes=[
            pltpu.VMEM((BLOCK, depth), BF16),
            pltpu.VMEM(w_query.shape, BF16),
            pltpu.VMEM(w_key.shape, BF16),
            pltpu.VMEM(w_value.shape, BF16),
            pltpu.SemaphoreType.DMA((NT,)),
            pltpu.SemaphoreType.DMA((4,)),
        ],
        compiler_params=pltpu.CompilerParams(vmem_limit_bytes=58 * MIB),
        cost_estimate=pl.CostEstimate(
            flops=2 * BLOCK * depth * (query_width + 2 * HD), bytes_accessed=9 * 10**6, transcendentals=0
        ),
        name="project",
    )(z, slots, *shards, cosine, sine, w_query, w_key, w_value, bias)


def attention_kernel(picks, load, split, passed, info_ref, q_ref, bias_ref, *refs):
    if load:
        wo_hbm, pool_hbm, handed_hbm, *refs = refs
        kv_ref, att_ref, wo_ref, wo_sem, kv_sem = refs[-5:]
        out_refs = refs[passed : -5]
    else:
        wo_hbm, kv_ref, *refs = refs
        *out_refs, att_ref, wo_ref, wo_sem = refs[passed:]
    z = info_ref[0]
    take = info_ref[1]

    def cache_copy(n, source):
        part = pl.ds(pl.multiple_of(n * CHROWS, CHROWS), CHROWS)
        return pltpu.make_async_copy(source.at[part], kv_ref.at[part], kv_sem.at[n])

    if load:

        @pl.when(take != 0)
        def _():
            for n in range(NCH):
                cache_copy(n, handed_hbm).start()

        @pl.when(take == 0)
        def _():
            for n in range(NCH):
                cache_copy(n, pool_hbm).start()

    wo_copy = pltpu.make_async_copy(wo_hbm, wo_ref, wo_sem)
    wo_copy.start()
    places = [lax.rem(z + pick, NT) for pick in picks]
    rows = HEADS * SHARD
    queries = jnp.concatenate([q_ref[pl.ds(pl.multiple_of(place * rows, rows), rows)] for place in places], axis=0)

    def scores(keys):
        return lax.dot_general(queries, keys, (((1,), (1,)), ((), ())), preferred_element_type=F32)

    def new_scores():
        block = scores(q_ref[NEW_KEYS])
        place = lax.broadcasted_iota(jnp.int32, (TILE, BLOCK), 0)
        row = place % SHARD + SHARD * jnp.where(place < TILE // 2, places[0], places[1])
        column = lax.broadcasted_iota(jnp.int32, (TILE, BLOCK), 1)
        return jnp.where(column <= row, block, MASKED)

    def stored_scores(at):
        at = pl.multiple_of(at, KBLK)
        return scores(kv_ref[pl.ds(at, KBLK), :HD]) + bias_ref[:, pl.ds(at, KBLK)]

    def fold(block, values, row_max, total, sums):
        lanes = [slice(c * HD, (c + 1) * HD) for c in range(block.shape[1] // HD)]
        top = block[:, lanes[0]]
        for lane in lanes[1:]:
            top = jnp.maximum(top, block[:, lane])
        raised = jnp.maximum(row_max, jnp.max(top, axis=1, keepdims=True))
        keep = jnp.exp2((row_max - raised) * EXP_SCALE)
        e = jnp.exp2((block - raised) * EXP_SCALE)
        total = total * keep
        for lane in lanes:
            total = total + e[:, lane]
        return raised, total, sums * keep + jnp.dot(e.astype(BF16), values, preferred_element_type=F32)

    def chunk(c, carry):
        base = pl.multiple_of(c * CHROWS, CHROWS)
        if load:
            cache_copy(c, pool_hbm).wait()
        block = stored_scores(base)
        for n in range(CHROWS // KBLK):
            following = stored_scores(base + (n + 1) * KBLK) if (n + 1) * KBLK < CHROWS else None
            values = kv_ref[pl.ds(pl.multiple_of(base + n * KBLK, KBLK), KBLK), HD:]
            carry = fold(block, values, *carry)
            block = following
        return carry

    zeros = jnp.zeros((TILE, HD), F32)
    carry = fold(new_scores(), q_ref[NEW_VALUES], jnp.full((TILE, 1), MASKED, F32), zeros, zeros)
    if 1 in picks:
        carry = lax.fori_loop(0, NCH, chunk, carry)
    else:
        for c in range(NCH):
            carry = chunk(c, carry)
    _, total, sums = carry
    attended = (sums / jnp.sum(total, axis=1, keepdims=True)).astype(BF16)
    for half in range(2):
        for n in range(HEADS):
            at = half * HEADS * SHARD + n * SHARD
            to = half * SHARD
            att_ref[to : to + SHARD, n * HD : (n + 1) * HD] = attended[at : at + SHARD, :]
    wo_copy.wait()
    product = jnp.dot(att_ref[...], wo_ref[...], preferred_element_type=F32).astype(BF16)
    if split:
        columns = product.shape[1] // 2
        out_refs[0][...] = product[:SHARD, :columns]
        out_refs[1][...] = product[:SHARD, columns:]
        out_refs[2][...] = product[SHARD:]
    else:
        out_refs[0][...] = product[:SHARD]
        out_refs[1][...] = product[SHARD:]


def attend(info, picks, projected, bias, w_output, *held, split=False, after=()):
    load = len(held) == 2
    width = w_output.shape[1]
    part = lambda columns: jax.ShapeDtypeStruct((SHARD, columns), BF16)
    out_shape = [part(width // 2), part(width // 2), part(width)] if split else [part(width)] * 2
    scratch = [pltpu.VMEM((2 * SHARD, HEADS * HD), BF16), pltpu.VMEM(w_output.shape, BF16), pltpu.SemaphoreType.DMA]
    if load:
        scratch += [pltpu.SemaphoreType.DMA((NCH,))]
    extra = [jax.ShapeDtypeStruct((PREFIX, 2 * HD), BF16)] if load else []
    return pl.pallas_call(
        functools.partial(attention_kernel, picks, load, split, len(after)),
        out_shape=out_shape + extra,
        in_specs=[SMEM, VMEM, VMEM, HBM] + ([HBM, HBM] if load else [VMEM]) + [ANY] * len(after),
        out_specs=[VMEM] * len(out_shape + extra),
        scratch_shapes=scratch,
        compiler_params=pltpu.CompilerParams(vmem_limit_bytes=(46 if load else 24) * MIB),
        cost_estimate=pl.CostEstimate(
            flops=8 * TILE * KEYS * HD, bytes_accessed=9 * 10**6, transcendentals=TILE * KEYS
        ),
        name="attend",
    )(info, projected, bias, w_output, *held, *after)


def plus(a, b):
    return a.astype(F32) + b.astype(F32)


def widen_kernel(up_ref, down_ref, from_left_ref, from_right_ref, up_out, down_out):
    half = from_left_ref.shape[1]
    up_out[:, :half] = plus(up_ref[:, :half], from_left_ref[...]).astype(BF16)
    up_out[:, half:] = up_ref[:, half:]
    down_out[:, :half] = down_ref[:, :half]
    down_out[:, half:] = plus(down_ref[:, half:], from_right_ref[...]).astype(BF16)


def add_kernel(up_ref, down_ref, from_left_ref, from_right_ref, up_out, down_out):
    up_out[...] = plus(up_ref[...], from_left_ref[...]).astype(BF16)
    down_out[...] = plus(down_ref[...], from_right_ref[...]).astype(BF16)


def last_kernel(rows_ref, part_ref, from_left_ref, from_right_ref, out_ref):
    branch = part_ref[...].astype(F32) + plus(from_left_ref[...], from_right_ref[...])
    out_ref[...] = (rows_ref[...].astype(F32) + branch).astype(BF16)


def combine(kernel, outputs, name, *arrays):
    shape = jax.ShapeDtypeStruct(arrays[0].shape, BF16)
    return pl.pallas_call(
        kernel,
        out_shape=[shape] * outputs,
        in_specs=[VMEM] * len(arrays),
        out_specs=[VMEM] * outputs,
        compiler_params=pltpu.CompilerParams(vmem_limit_bytes=8 * MIB),
        cost_estimate=pl.CostEstimate(flops=10**6, bytes_accessed=2 * 10**6, transcendentals=0),
        name=name,
    )(*arrays)


def pick_kernel(source_ref, pages_ref, out_ref):
    for k in range(out_ref.shape[0]):
        out_ref[k] = pages_ref[source_ref[k]]


def pick_pages(sources, pages, count):
    return pl.pallas_call(
        pick_kernel,
        out_shape=jax.ShapeDtypeStruct((count,) + pages.shape[1:], BF16),
        in_specs=[SMEM, VMEM],
        out_specs=VMEM,
        compiler_params=pltpu.CompilerParams(vmem_limit_bytes=4 * MIB),
        cost_estimate=pl.CostEstimate(flops=0, bytes_accessed=4 * 10**5, transcendentals=0),
        name="pick_pages",
    )(sources, pages)


def local(
    hidden,
    norm_gain,
    w_query,
    w_key,
    w_value,
    w_output,
    prefix_pool,
    page_table,
    prefix_len,
    source,
    decode_owner,
):
    groups = lax.axis_size("group")
    group = lax.axis_index("group")
    z = lax.axis_index("tensor")
    lower = (group + groups - 1) % groups
    take = source[group] == lower
    take_flag = take.astype(jnp.int32)

    sent_rows = hidden[0, 1]
    sent_table = page_table[0, 1]
    handed_rows = shift(sent_rows, "group", 1)
    handed_table = shift(sent_table, "group", 1)
    pages = prefix_pool.shape[0] // 2
    slot = second_slot(prefix_pool, sent_rows, sent_table)
    rows, normed, slot = choose_and_norm(
        take_flag[None], hidden[0, 0], handed_rows, norm_gain[None], slot, handed_table[None]
    )
    handed = shift(slot, "group", 1).reshape(PREFIX, 2 * HD)

    up, down = [normed], [normed]
    for _ in range(NT // 2 - 1):
        up.append(shift(up[-1], "tensor", 1))
        down.append(shift(down[-1], "tensor", -1))
    prefix_len, decode_owner, handed_table = later((prefix_len, decode_owner, handed_table[None]), up[1])
    count = jnp.where(take, prefix_len[lower, 1], prefix_len[group, 0])
    half = SHARD // 2
    opposite = jnp.concatenate([shift(up[-1][:half], "tensor", 1), shift(down[-1][half:], "tensor", -1)], axis=0)
    shards = down + [opposite] + up[:0:-1]

    table = jnp.where(take, handed_table[0], page_table[0, 0])
    order = jnp.arange(pages, dtype=jnp.int32)
    place = jnp.sum(jnp.where(table[:, None] == order[None, :], order[:, None], 0), axis=0)
    position = place[:, None] * PAGE + jnp.arange(PAGE, dtype=jnp.int32)[None, :]
    bias = jnp.where(position < count, 0.0, MASKED).astype(F32).reshape(1, PREFIX)

    positions = (count + jnp.arange(BLOCK, dtype=jnp.int32)).astype(F32)
    frequency = THETA ** (-(jnp.arange(HD // 2, dtype=F32) * 2.0) / HD)
    angles = positions[:, None] * frequency
    cosine = jnp.cos(angles)
    sine = jnp.sin(angles)
    cosine = jnp.concatenate([cosine, cosine], axis=1)
    sine = jnp.concatenate([-sine, sine], axis=1)

    page_count = BLOCK // PAGE
    ids = jnp.arange(page_count, dtype=jnp.int32)
    same = jnp.logical_and(decode_owner[:, :, None] == decode_owner[:, None, :], ids[None, None, :] < ids[None, :, None])
    ranks = jnp.sum(same.astype(jnp.int32), axis=-1)
    slots = decode_owner[group] * SLOTS + ranks[group]
    mine = decode_owner == group
    senders = jnp.arange(groups, dtype=jnp.int32)[:, None] * SLOTS + ranks
    sources = jnp.sum(jnp.where(mine, senders, 0), axis=0)
    projected, outgoing = project(
        z[None], slots, groups * SLOTS, shards, cosine, sine, w_query, w_key, w_value, bias
    )
    incoming = lax.all_to_all(outgoing, "group", split_axis=0, concat_axis=0, tiled=True)
    kv_pool = pick_pages(sources, incoming, page_count)

    info = jnp.stack([z.astype(jnp.int32), take_flag])
    pool = prefix_pool.reshape(2 * PREFIX, 2 * HD)

    work = (projected, bias, w_output)
    left, right, own_part, cache = attend(info, (4, 0), *work, pool, handed, split=True)
    ups, downs = {}, {}
    ups[3], downs[3] = attend(info, (3, 5), *work, cache)
    ups[2], downs[2], cache = attend(info, (2, 6), *work, pool, handed, after=(incoming,))
    ups[1], downs[1] = attend(info, (1, 7), *work, cache)
    going_up, going_down = shift(left, "tensor", 1), shift(right, "tensor", -1)
    for distance in (3, 2, 1):
        kernel = widen_kernel if distance == 3 else add_kernel
        going_up, going_down = combine(kernel, 2, "add_parts", ups[distance], downs[distance], going_up, going_down)
        going_up, going_down = shift(going_up, "tensor", 1), shift(going_down, "tensor", -1)
    (layer_out,) = combine(last_kernel, 1, "add_rows", rows, own_part, going_up, going_down)
    return (layer_out, kv_pool)


def solution(mesh):
    return jax.shard_map(
        local,
        mesh=mesh,
        in_specs=(
            P("group", None, "tensor", None),
            P(),
            P(None, "tensor"),
            P(None, "tensor"),
            P(None, "tensor"),
            P("tensor", None),
            P("group", None, "tensor"),
            P("group", None, None),
            P(),
            P(),
            P(),
        ),
        out_specs=(P(("group", "tensor"), None), P("group", None, "tensor")),
        check_vma=False,
    )
```
